32 devices in a mesh: groups: 2 (over x), rows: 16 (over z, y, core).
Axes of the slice: x: 2, y: 2, z: 4, core: 2. Of those that a mesh axis runs over, the one named last changes fastest.
Arguments:
- local_tiles: bfloat16 [8192, 128, 128], P(('groups', 'rows')), parts along dimension 0, may hold values from 0 to 1, as said below
- local_row: int32 [8192], P(('groups', 'rows')), parts along dimension 0, may hold values from 0 to 15, as said below
- local_col: int32 [8192], P(('groups', 'rows')), parts along dimension 0, may hold values from 0 to 15, as said below
- local_count: int32 [32], P(('groups', 'rows')), parts along dimension 0, may hold values from 128 to 256, as said below
- remote_tiles: bfloat16 [512, 4, 128, 128], P(('groups', 'rows')), parts along dimension 0, may hold values from 0 to 1, as said below
- remote_row: int32 [512, 4], P(('groups', 'rows')), parts along dimension 0, may hold values from 0 to 15, as said below
- remote_col: int32 [512, 4], P(('groups', 'rows')), parts along dimension 0, may hold values from 0 to 15, as said below
- remote_count: int32 [512], P(('groups', 'rows')), parts along dimension 0, may hold values from 0 to 4, as said below
- start_basis: float32 [128, 32768], P('groups', 'rows'), parts along dimension 0, may hold values from -6 to 6
- start_dir: float32 [128, 32768], P('groups', 'rows'), parts along dimension 0, may hold values from -4 to 4
- coeffs: float32 [4, 64, 192], P('groups'), parts along dimension 0, may hold values from -4 to 4, as said below
Outputs:
- ortho_out: float32 [128, 32768], P('groups', 'rows'), parts along dimension 0
- residual_out: float32 [128, 32768], P('groups', 'rows'), parts along dimension 0
- projected_out: float32 [128, 64], P('groups'), parts along dimension 0
The draws below stay inside these ranges and needn't reach their ends.
There are 2 independent parts, one for each index of `groups`. The reference program is written for one: setup_inputs(seed, part) draws one part's arguments, and reference() takes and returns one part's arrays. A program takes and returns all parts, laid end to end along the dimension named above; each array names one. Nothing has to cross between parts.
Inputs may be any that keep to these rules, and one draw needn't show every extreme that they name: `local_tiles`: entries are 0 or between 0.25 and 1; slots past the live counts hold values that must be ignored. `remote_tiles`: entries are 0 or between 0.25 and 1; slots past the live counts hold values that must be ignored. `local_row`: block index on the owning device; slots 0 to 15 of each device hold its diagonal tiles. `local_col`: block index on the same device. `local_count`: some device has all 256 slots live in every draw. `remote_row`: block index on the owning device. `remote_col`: block index on the peer. `remote_count`: 0 toward the device itself, at least 1 toward every other peer; every device has some peer with exactly 4. `coeffs`: the basis part is the identity plus off-diagonal and diagonal perturbations of magnitude at most 0.15.
All inputs are finite; a program needn't handle non-finite values.
Results may differ from the reference program's by a relative error of at most 0.00086.
Values may be sent and summed in bfloat16 or wider, within the bound.
A program may use at most 192 MiB of HBM per device.

```python
import jax
import jax.numpy as jnp
from jax import lax

K = 64
BLOCK = 128
NB_DEV = 16
CAP = 4
ITERS = 2
LOC_DEV = 256
NODES = 32768
N_ROWS = 16


def tile_values(key, count):
    key_vals, key_mask = jax.random.split(key)
    values = jax.random.uniform(key_vals, (count, BLOCK, BLOCK), jnp.float32, 0.25, 1.0)
    present = (jax.random.randint(key_mask, (count, BLOCK, BLOCK), 0, 16) == 0).astype(jnp.float32)
    return (values * present).astype(jnp.bfloat16)


def draw_local_tiles(key, part):
    key = jax.random.fold_in(key, 1)
    return tile_values(key, N_ROWS * LOC_DEV)


def draw_remote_tiles(key, part):
    key = jax.random.fold_in(key, 2)
    return tile_values(key, N_ROWS * N_ROWS * CAP).reshape(N_ROWS * N_ROWS, CAP, BLOCK, BLOCK)


def block_list(key):
    others = jax.random.randint(key, (N_ROWS, LOC_DEV - NB_DEV), 0, NB_DEV)
    diagonal = jnp.broadcast_to(jnp.arange(NB_DEV, dtype=jnp.int32)[None, :], (N_ROWS, NB_DEV))
    return jnp.concatenate([diagonal, others.astype(jnp.int32)], axis=1).reshape(N_ROWS * LOC_DEV)


def draw_local_row(key, part):
    key = jax.random.fold_in(key, 3)
    return block_list(key)


def draw_local_col(key, part):
    key = jax.random.fold_in(key, 4)
    return block_list(key)


def draw_local_count(key, part):
    key = jax.random.fold_in(key, 5)
    key_a, key_b = jax.random.split(key)
    counts = jax.random.randint(key_a, (N_ROWS,), LOC_DEV // 2, LOC_DEV + 1)
    fullest = jax.random.randint(key_b, (), 0, N_ROWS)
    counts = jnp.where(jnp.arange(N_ROWS) == fullest, LOC_DEV, counts)
    return counts.astype(jnp.int32)


def draw_remote_row(key, part):
    key = jax.random.fold_in(key, 6)
    return jax.random.randint(key, (N_ROWS * N_ROWS, CAP), 0, NB_DEV).astype(jnp.int32)


def draw_remote_col(key, part):
    key = jax.random.fold_in(key, 7)
    return jax.random.randint(key, (N_ROWS * N_ROWS, CAP), 0, NB_DEV).astype(jnp.int32)


def draw_remote_count(key, part):
    key = jax.random.fold_in(key, 8)
    key_a, key_b = jax.random.split(key)
    counts = jax.random.randint(key_a, (N_ROWS, N_ROWS), 1, CAP + 1)
    offset = jax.random.randint(key_b, (N_ROWS,), 1, N_ROWS)
    owners = jnp.arange(N_ROWS)
    busiest = owners[None, :] == ((owners + offset) % N_ROWS)[:, None]
    itself = owners[None, :] == owners[:, None]
    counts = jnp.where(busiest, CAP, jnp.where(itself, 0, counts))
    return counts.reshape(N_ROWS * N_ROWS).astype(jnp.int32)


def draw_coeffs(key, part):
    key = jax.random.fold_in(key, 9)
    key_x, key_r, key_p = jax.random.split(key, 3)
    scale = K ** (-0.5)
    basis_part = jnp.eye(K, dtype=jnp.float32)[None] + 0.3 * scale * jnp.clip(jax.random.normal(key_x, (ITERS, K, K), jnp.float32), -4.0, 4.0)
    resid_part = scale * jnp.clip(jax.random.normal(key_r, (ITERS, K, K), jnp.float32), -4.0, 4.0)
    dir_part = 0.5 * scale * jnp.clip(jax.random.normal(key_p, (ITERS, K, K), jnp.float32), -4.0, 4.0)
    return jnp.concatenate([basis_part, resid_part, dir_part], axis=2)


def shard_levels(stream_key, shape, cuts, least, largest):
    gain = 1.0
    for position, shards_of in cuts:
        heights = jax.random.uniform(jax.random.fold_in(jax.random.fold_in(stream_key, 6), position), (shards_of,), jnp.float32, least / len(cuts), largest / len(cuts))
        gain = gain * jnp.repeat(jnp.exp(heights), shape[position] // shards_of).reshape((-1,) + (1,) * (len(shape) - 1 - position))
    return gain


def scatter_about(own_key, dims, width, limit, shards=(), held_as=jnp.bfloat16):
    values = jax.random.normal(own_key, dims, jnp.float32) * width
    if len(shards) > 0:
        values = shard_levels(own_key, dims, shards, -0.22, 0.18) * values
    return jnp.clip(values, min=-limit, max=limit).astype(held_as)


def setup_inputs(seed: int = 0, part: int = 0) -> dict:
    keys = jax.random.split(jax.random.key(seed), 12)
    own_keys = jax.random.split(jax.random.fold_in(keys[11], part), 12)
    return {
        "local_tiles": draw_local_tiles(jax.random.fold_in(jax.random.fold_in(keys[11], part), 71), part),
        "local_row": draw_local_row(jax.random.fold_in(jax.random.fold_in(keys[11], part), 71), part),
        "local_col": draw_local_col(jax.random.fold_in(jax.random.fold_in(keys[11], part), 71), part),
        "local_count": draw_local_count(jax.random.fold_in(jax.random.fold_in(keys[11], part), 71), part),
        "remote_tiles": draw_remote_tiles(jax.random.fold_in(jax.random.fold_in(keys[11], part), 71), part),
        "remote_row": draw_remote_row(jax.random.fold_in(jax.random.fold_in(keys[11], part), 71), part),
        "remote_col": draw_remote_col(jax.random.fold_in(jax.random.fold_in(keys[11], part), 71), part),
        "remote_count": draw_remote_count(jax.random.fold_in(jax.random.fold_in(keys[11], part), 71), part),
        "start_basis": scatter_about(own_keys[8], (K, NODES), 1.0, 6.0, ((1, 16),), jnp.float32),
        "start_dir": scatter_about(own_keys[9], (K, NODES), 0.3, 4.0, ((1, 16),), jnp.float32),
        "coeffs": draw_coeffs(jax.random.fold_in(jax.random.fold_in(keys[11], part), 71), part),
    }


highest = lax.Precision.HIGHEST

def reference(local_tiles, local_row, local_col, local_count, remote_tiles, remote_row, remote_col, remote_count, start_basis, start_dir, coeffs):
    tile_grid = local_tiles.reshape(N_ROWS, LOC_DEV, BLOCK, BLOCK)
    row_grid = local_row.reshape(N_ROWS, LOC_DEV)
    col_grid = local_col.reshape(N_ROWS, LOC_DEV)
    live_local = (jnp.arange(LOC_DEV)[None, :] < local_count[:, None]).astype(jnp.float32)
    far_grid = remote_tiles.reshape(N_ROWS, N_ROWS, CAP, BLOCK, BLOCK)
    far_rows = remote_row.reshape(N_ROWS, N_ROWS, CAP)
    far_cols = remote_col.reshape(N_ROWS, N_ROWS, CAP)
    live_far = (jnp.arange(CAP)[None, None, :] < remote_count.reshape(N_ROWS, N_ROWS)[:, :, None]).astype(jnp.float32)
    peer_ids = jnp.arange(N_ROWS)

    def degree_step(summed, device):
        tiles_now = tile_grid[device].astype(jnp.float32)
        weight = live_local[device][:, None]
        summed = summed.at[device, row_grid[device]].add(jnp.sum(tiles_now, axis=2) * weight)
        summed = summed.at[device, col_grid[device]].add(jnp.sum(tiles_now, axis=1) * weight)
        far_now = far_grid[device].astype(jnp.float32)
        far_weight = live_far[device][:, :, None]
        summed = summed.at[device, far_rows[device]].add(jnp.sum(far_now, axis=3) * far_weight)
        summed = summed.at[peer_ids[:, None], far_cols[device]].add(jnp.sum(far_now, axis=2) * far_weight)
        return (summed, None)
    deg_init = jnp.zeros((N_ROWS, NB_DEV, BLOCK), jnp.float32)
    deg_sum, unused = lax.scan(degree_step, deg_init, jnp.arange(N_ROWS))
    degree = 0.5 * deg_sum.reshape(NODES)

    def apply_operator(basis):
        basis_bf = basis.astype(jnp.bfloat16)
        blocks_bf = basis_bf.reshape(K, N_ROWS, NB_DEV, BLOCK).transpose(1, 2, 0, 3)

        def product_step(summed, device):
            tiles_now = tile_grid[device].astype(jnp.float32)
            weight = live_local[device][:, None, None]
            own = blocks_bf[device].astype(jnp.float32)
            near_part = jnp.einsum('tij,tkj->tki', tiles_now, own[col_grid[device]]) * weight
            summed = summed.at[device, row_grid[device]].add(near_part)
            back_part = jnp.einsum('tji,tkj->tki', tiles_now, own[row_grid[device]]) * weight
            summed = summed.at[device, col_grid[device]].add(back_part)
            far_now = far_grid[device].astype(jnp.float32)
            far_weight = live_far[device][:, :, None, None]
            fetched = blocks_bf[peer_ids[:, None], far_cols[device]].astype(jnp.float32)
            ahead_part = jnp.einsum('ecij,eckj->ecki', far_now, fetched) * far_weight
            summed = summed.at[device, far_rows[device]].add(ahead_part)
            returned = jnp.einsum('ecji,eckj->ecki', far_now, own[far_rows[device]]) * far_weight
            summed = summed.at[peer_ids[:, None], far_cols[device]].add(returned)
            return (summed, None)
        init = jnp.zeros((N_ROWS, NB_DEV, K, BLOCK), jnp.float32)
        summed, unused_two = lax.scan(product_step, init, jnp.arange(N_ROWS))
        summed = summed.transpose(2, 0, 1, 3).reshape(K, NODES)
        return degree[None, :] * basis - 0.5 * summed
    basis = start_basis
    direction = start_dir
    identity = jnp.eye(K, dtype=jnp.float32)
    for iteration in range(ITERS + 1):
        image = apply_operator(basis)
        gram_now = jnp.dot(basis.astype(jnp.float32), basis.T.astype(jnp.float32), precision=highest, preferred_element_type=jnp.float32) / NODES
        cross_now = jnp.dot(image.astype(jnp.float32), basis.T.astype(jnp.float32), precision=highest, preferred_element_type=jnp.float32) / NODES
        lower_chol = jnp.linalg.cholesky(gram_now)
        lower_inv = jax.scipy.linalg.solve_triangular(lower_chol, identity, lower=True)
        ortho = jnp.dot(lower_inv.astype(jnp.float32), basis.astype(jnp.float32), precision=highest, preferred_element_type=jnp.float32)
        image_ortho = jnp.dot(lower_inv.astype(jnp.float32), image.astype(jnp.float32), precision=highest, preferred_element_type=jnp.float32)
        projected = jnp.dot(jnp.dot(lower_inv.astype(jnp.float32), cross_now.astype(jnp.float32), precision=highest, preferred_element_type=jnp.float32).astype(jnp.float32), lower_inv.T.astype(jnp.float32), precision=highest, preferred_element_type=jnp.float32)
        residual = (image_ortho - jnp.dot(projected.astype(jnp.float32), ortho.astype(jnp.float32), precision=highest, preferred_element_type=jnp.float32)) / (1.0 + degree)[None, :]
        if iteration < ITERS:
            coeff_now = coeffs[iteration]
            direction = jnp.dot(coeff_now[:, K:2 * K].astype(jnp.float32), residual.astype(jnp.float32), precision=highest, preferred_element_type=jnp.float32) + jnp.dot(coeff_now[:, 2 * K:].astype(jnp.float32), direction.astype(jnp.float32), precision=highest, preferred_element_type=jnp.float32)
            basis = jnp.dot(coeff_now[:, :K].astype(jnp.float32), ortho.astype(jnp.float32), precision=highest, preferred_element_type=jnp.float32) + direction
    return (ortho, residual, projected)
```

```python
import functools

import jax
import jax.numpy as jnp
from jax import lax
from jax.experimental import pallas as pl
from jax.experimental.pallas import tpu as pltpu
from jax.sharding import PartitionSpec as P

highest = lax.Precision.HIGHEST
f32 = jnp.float32
bf16 = jnp.bfloat16
NT = (((1,), (1,)), ((), ()))
MIB = 1024 * 1024


def dot_nt(a, b, precision=None):
    return lax.dot_general(a, b, NT, precision=precision, preferred_element_type=f32)


def dot_nn(a, b, precision=None):
    return jnp.dot(a, b, precision=precision, preferred_element_type=f32)


def fold(square):
    half = square.shape[0] // 2
    return jnp.concatenate([square[:half], square[half:]], axis=1)


def unfold(folded):
    half = folded.shape[1] // 2
    return jnp.concatenate([folded[:, :half], folded[:, half:]], axis=0)


def peer_barrier(me, size):
    barrier = pltpu.get_barrier_semaphore()
    for k in range(1, size):
        pl.semaphore_signal(
            barrier, inc=1, device_id={"rows": lax.rem(me + k, size)}, device_id_type=pl.DeviceIdType.MESH
        )
    pl.semaphore_wait(barrier, size - 1)


def ordered_sum(me, size, part_ref, buf):
    buf[0] = part_ref[...]
    total = buf[me]
    for p in range(1, size):
        total = total + buf[lax.rem(me - p + size, size)]
    return total


def remote(src, dst, send, recv, target):
    return pltpu.make_async_remote_copy(
        src_ref=src,
        dst_ref=dst,
        send_sem=send,
        recv_sem=recv,
        device_id={"rows": target},
        device_id_type=pl.DeviceIdType.MESH,
    )


def dense_kernel(per_step, count_ref, row_ref, col_ref, tiles_ref, dense_ref, acc):
    step = pl.program_id(0)
    edge = tiles_ref.shape[1]

    @pl.when(step == 0)
    def _():
        acc[...] = jnp.zeros_like(acc)

    for t in range(per_step):
        slot = step * per_step + t

        @pl.when(slot < count_ref[0])
        def _():
            r = pl.multiple_of(row_ref[slot] * edge, edge)
            c = pl.multiple_of(col_ref[slot] * edge, edge)
            acc[pl.ds(r, edge), pl.ds(c, edge)] += tiles_ref[t].astype(f32)

    @pl.when(step == pl.num_programs(0) - 1)
    def _():
        dense_ref[...] = acc[...].astype(bf16)


def dense_local(count, row, col, tiles, nodes):
    slots, edge, _ = tiles.shape
    per_step = 16
    return pl.pallas_call(
        functools.partial(dense_kernel, per_step),
        grid_spec=pltpu.PrefetchScalarGridSpec(
            num_scalar_prefetch=3,
            grid=(slots // per_step,),
            in_specs=[pl.BlockSpec((per_step, edge, edge), lambda i, *_: (i, 0, 0))],
            out_specs=pl.BlockSpec((nodes, nodes), lambda i, *_: (0, 0)),
            scratch_shapes=[pltpu.VMEM((nodes, nodes), f32)],
        ),
        out_shape=jax.ShapeDtypeStruct((nodes, nodes), bf16),
        compiler_params=pltpu.CompilerParams(vmem_limit_bytes=44 * MIB),
        cost_estimate=pl.CostEstimate(flops=10**9, bytes_accessed=40 * MIB, transcendentals=0),
        name="dense_local",
    )(count, row, col, tiles)


def gather_kernel(size, node_total, x_ref, gram_ref, xg_ref, inv_ref, gbuf, g_send, g_recv, own_send, own_sem,
                  z_recv, y_recv, s_recv, f_send, s_send):
    me = lax.axis_index("rows")
    deep = size // 4
    core = lax.rem(me, 2)
    mid = lax.rem(me // 2, 2)
    sib = me + 1 - 2 * core
    ynb = me + 2 - 4 * mid

    def back(base, k):
        return lax.rem(base - 4 * k + size, size)

    peer_barrier(me, size)
    waits = []
    small = []
    for k in range(1, size):
        copy = remote(gram_ref, gbuf.at[k], g_send.at[k], g_recv.at[k], lax.rem(me + k, size))
        copy.start()
        small.append(copy)
    copy = remote(x_ref, xg_ref.at[me], own_send.at[0], y_recv.at[0], ynb)
    copy.start()
    waits.append(copy)
    for k in range(1, deep):
        copy = remote(x_ref, xg_ref.at[me], own_send.at[k], z_recv.at[k], lax.rem(me + 4 * k, size))
        copy.start()
        waits.append(copy)
    copy = remote(x_ref, xg_ref.at[me], own_send.at[deep], s_recv.at[0], sib)
    copy.start()
    waits.append(copy)
    own = pltpu.make_async_copy(x_ref, xg_ref.at[me], own_sem)
    own.start()

    for k in range(1, deep):
        src = back(me, k)
        remote(x_ref, xg_ref.at[src], own_send.at[k], z_recv.at[k], ynb).wait_recv()
        copy = remote(xg_ref.at[src], xg_ref.at[src], f_send.at[k], y_recv.at[k], ynb)
        copy.start()
        waits.append(copy)
        copy = remote(xg_ref.at[src], xg_ref.at[src], s_send.at[k], s_recv.at[k], sib)
        copy.start()
        waits.append(copy)

    for copy in small:
        copy.wait_recv()
    gram = unfold(ordered_sum(me, size, gram_ref, gbuf)) / node_total
    n = gram.shape[0]
    rows = lax.broadcasted_iota(jnp.int32, (n, 2 * n), 0)
    lanes = lax.broadcasted_iota(jnp.int32, (n, 2 * n), 1)
    unit = jnp.where(rows == lanes, 1.0, 0.0)
    both = jnp.where(lanes < n, unit, jnp.concatenate([gram, gram], axis=1))

    def eliminate(k, both):
        row = jnp.sum(jnp.where(rows == k, both, 0.0), axis=0, keepdims=True)
        col = jnp.sum(jnp.where(lanes == k + n, both, 0.0), axis=1, keepdims=True)
        pivot = jnp.sum(jnp.where(lanes[:1] == k + n, row, 0.0), axis=1, keepdims=True)
        scaled = row * (1.0 / pivot)
        return both - jnp.where(rows > k, col * scaled, 0.0)

    both = lax.fori_loop(0, n, eliminate, both)
    diag = jnp.sum(jnp.where(lanes == rows + n, both, 0.0), axis=1, keepdims=True)
    inv_ref[...] = (both * (1.0 / jnp.sqrt(diag)))[:, :n]

    for k in range(deep):
        src = back(ynb, k)
        remote(x_ref, xg_ref.at[src], own_send.at[0], y_recv.at[k], ynb).wait_recv()
        copy = remote(xg_ref.at[src], xg_ref.at[src], s_send.at[deep + k], s_recv.at[deep + k], sib)
        copy.start()
        waits.append(copy)
    other = sib + 2 - 4 * mid
    for k in range(deep):
        src = back(sib, k)
        remote(x_ref, xg_ref.at[src], own_send.at[0], s_recv.at[k], sib).wait_recv()
    for k in range(deep):
        src = back(other, k)
        remote(x_ref, xg_ref.at[src], own_send.at[0], s_recv.at[deep + k], sib).wait_recv()
    for copy in small + waits:
        copy.wait_send()
    own.wait()


def gather_basis(x_bf, gram_part, size, node_total):
    columns, nodes = x_bf.shape
    deep = size // 4
    dma = pltpu.SemaphoreType.DMA
    return pl.pallas_call(
        functools.partial(gather_kernel, size, float(node_total)),
        in_specs=[pl.BlockSpec(memory_space=pl.ANY), pl.BlockSpec(memory_space=pltpu.VMEM)],
        out_specs=[pl.BlockSpec(memory_space=pl.ANY), pl.BlockSpec(memory_space=pltpu.VMEM)],
        out_shape=[
            jax.ShapeDtypeStruct((size, columns, nodes), bf16),
            jax.ShapeDtypeStruct((columns, columns), f32),
        ],
        scratch_shapes=[
            pltpu.VMEM((size,) + gram_part.shape, f32),
            dma((size,)),
            dma((size,)),
            dma((deep + 1,)),
            dma,
            dma((deep,)),
            dma((deep,)),
            dma((2 * deep,)),
            dma((deep,)),
            dma((2 * deep,)),
        ],
        compiler_params=pltpu.CompilerParams(
            collective_id=0, has_side_effects=True, vmem_limit_bytes=16 * MIB
        ),
        name="gather_basis",
    )(x_bf, gram_part)


def sum_kernel(size, part_ref, out_ref, buf, send, recv):
    me = lax.axis_index("rows")
    peer_barrier(me, size)
    copies = []
    for k in range(1, size):
        copy = remote(part_ref, buf.at[k], send.at[k], recv.at[k], lax.rem(me + k, size))
        copy.start()
        copies.append(copy)
    for copy in copies:
        copy.wait()
    out_ref[...] = ordered_sum(me, size, part_ref, buf)


def sum_rows(part, size):
    dma = pltpu.SemaphoreType.DMA
    return pl.pallas_call(
        functools.partial(sum_kernel, size),
        in_specs=[pl.BlockSpec(memory_space=pltpu.VMEM)],
        out_specs=pl.BlockSpec(memory_space=pltpu.VMEM),
        out_shape=jax.ShapeDtypeStruct(part.shape, f32),
        scratch_shapes=[pltpu.VMEM((size,) + part.shape, f32), dma((size,)), dma((size,))],
        compiler_params=pltpu.CompilerParams(
            collective_id=1, has_side_effects=True, vmem_limit_bytes=16 * MIB
        ),
        name="sum_rows",
    )(part)


def apply_kernel(first, slots, own_src, own_dst, in_src, in_dst, *refs):
    if first:
        dense_ref, own_ref, in_ref, xg_ref, x_ref, image_ref, cross_ref, degree_ref, acc, far = refs
    else:
        dense_ref, own_ref, in_ref, xg_ref, x_ref, degree_ref, image_ref, cross_ref, acc, far = refs
    step = pl.program_id(0)
    columns, nodes = x_ref.shape
    edge = own_ref.shape[1]
    chunk = dense_ref.shape[0]

    def with_ones(x):
        if first:
            return jnp.concatenate([x, jnp.ones((16, x.shape[1]), bf16)], axis=0)
        return x

    @pl.when(step == 0)
    def _():
        acc[...] = jnp.zeros_like(acc)
        far[...] = jnp.zeros_like(far)

    x_all = with_ones(x_ref[...].astype(bf16))
    here = pl.ds(pl.multiple_of(step * chunk, chunk), chunk)
    x_here = with_ones(x_ref[:, here].astype(bf16))
    dense = dense_ref[...]
    acc[...] += dot_nn(x_here, dense)
    acc[:, here] += dot_nt(x_all, dense)

    count = own_ref.shape[0]
    blocks = nodes // edge
    for tiles_ref, src_ref, dst_ref, dot in (
        (own_ref, own_src, own_dst, dot_nt),
        (in_ref, in_src, in_dst, dot_nn),
    ):
        products = []
        for t in range(count):
            slot = step * count + t
            at = pl.ds(pl.multiple_of(src_ref[slot] * edge, edge), edge)
            products.append(dot(with_ones(xg_ref[slot // slots, :, at]), tiles_ref[t]))
        for t in range(count):
            far[dst_ref[step * count + t]] += products[t]

    @pl.when(step == pl.num_programs(0) - 1)
    def _():
        for b in range(blocks):
            at = slice(b * edge, (b + 1) * edge)
            both = acc[:, at] + far[b]
            if first:
                degree = 0.5 * both[columns : columns + 1]
                degree_ref[:, at] = jnp.broadcast_to(degree, (8, edge))
            else:
                degree = degree_ref[:1, at]
            image_ref[:, at] = degree * x_ref[:, at] - 0.5 * both[:columns]
        cross_ref[...] = fold(dot_nt(image_ref[...], x_ref[...], highest))


def apply_operator(first, slots, index, dense, own_tiles, in_tiles, xg, x, degree):
    columns, nodes = x.shape
    edge = own_tiles.shape[1]
    steps = 8
    chunk = nodes // steps
    count = own_tiles.shape[0] // steps
    whole = lambda shape: pl.BlockSpec(shape, lambda i, *_: (0,) * len(shape))
    rows = columns + 16 if first else columns
    tile_spec = pl.BlockSpec((count, edge, edge), lambda i, *_: (i, 0, 0))
    degree_shape = (8, nodes)
    in_specs = [
        pl.BlockSpec((chunk, nodes), lambda i, *_: (i, 0)),
        tile_spec,
        tile_spec,
        whole(xg.shape),
        whole(x.shape),
    ]
    out_specs = [whole(x.shape), whole((columns // 2, 2 * columns))]
    out_shape = [
        jax.ShapeDtypeStruct(x.shape, f32),
        jax.ShapeDtypeStruct((columns // 2, 2 * columns), f32),
    ]
    operands = [dense, own_tiles, in_tiles, xg, x]
    if first:
        out_specs.append(whole(degree_shape))
        out_shape.append(jax.ShapeDtypeStruct(degree_shape, f32))
    else:
        in_specs.append(whole(degree_shape))
        operands.append(degree)
    return pl.pallas_call(
        functools.partial(apply_kernel, first, slots),
        grid_spec=pltpu.PrefetchScalarGridSpec(
            num_scalar_prefetch=4,
            grid=(steps,),
            in_specs=in_specs,
            out_specs=out_specs,
            scratch_shapes=[
                pltpu.VMEM((rows, nodes), f32),
                pltpu.VMEM((nodes // edge + 1, rows, edge), f32),
            ],
        ),
        out_shape=out_shape,
        compiler_params=pltpu.CompilerParams(vmem_limit_bytes=44 * MIB),
        name="apply_operator",
    )(*index, *operands)


def update_kernel(last, node_total, inv_ref, cross_ref, image_ref, x_ref, degree_ref, *refs):
    inv = inv_ref[...]
    n = inv.shape[0]
    cross = unfold(cross_ref[...]) / node_total
    projected = dot_nt(dot_nn(inv, cross, highest), inv, highest)
    scale = 1.0 / (1.0 + degree_ref[:1, :])
    x = x_ref[...]
    p_inv = dot_nn(projected, inv, highest)
    if last:
        ortho_ref, residual_ref, projected_ref = refs
        ortho_ref[...] = dot_nn(inv, x, highest)
        residual_ref[...] = (dot_nn(inv, image_ref[...], highest) - dot_nn(p_inv, x, highest)) * scale
        projected_ref[...] = projected
    else:
        coeff_ref, dir_ref, x_out, bf_out, dir_out, gram_out = refs
        c_x, c_r, c_p = coeff_ref[:, :n], coeff_ref[:, n : 2 * n], coeff_ref[:, 2 * n :]
        m_image = dot_nn(c_r, inv, highest)
        m_x = dot_nn(c_r, p_inv, highest)
        m_basis = dot_nn(c_x, inv, highest)
        direction = (dot_nn(m_image, image_ref[...], highest) - dot_nn(m_x, x, highest)) * scale
        direction = direction + dot_nn(c_p, dir_ref[...], highest)
        basis = dot_nn(m_basis, x, highest) + direction
        dir_out[...] = direction
        x_out[...] = basis
        bf_out[...] = basis.astype(bf16)
        gram_out[...] = fold(dot_nt(basis, basis, highest))


def update(last, node_total, inv, cross, image, x, degree, coeff=None, direction=None):
    columns, nodes = x.shape
    big = jax.ShapeDtypeStruct((columns, nodes), f32)
    if last:
        shapes = [big, big, jax.ShapeDtypeStruct((columns, columns), f32)]
        operands = (inv, cross, image, x, degree)
    else:
        shapes = [
            big,
            jax.ShapeDtypeStruct((columns, nodes), bf16),
            big,
            jax.ShapeDtypeStruct((columns // 2, 2 * columns), f32),
        ]
        operands = (inv, cross, image, x, degree, coeff, direction)
    vmem = pl.BlockSpec(memory_space=pltpu.VMEM)
    return pl.pallas_call(
        functools.partial(update_kernel, last, float(node_total)),
        in_specs=[vmem] * len(operands),
        out_specs=[vmem] * len(shapes),
        out_shape=shapes,
        compiler_params=pltpu.CompilerParams(vmem_limit_bytes=32 * MIB),
        name="update",
    )(*operands)


def start_kernel(x_ref, bf_out, gram_out):
    x = x_ref[...]
    bf_out[...] = x.astype(bf16)
    gram_out[...] = fold(dot_nt(x, x, highest))


def start(x):
    columns, nodes = x.shape
    vmem = pl.BlockSpec(memory_space=pltpu.VMEM)
    return pl.pallas_call(
        start_kernel,
        in_specs=[vmem],
        out_specs=[vmem] * 2,
        out_shape=[
            jax.ShapeDtypeStruct((columns, nodes), bf16),
            jax.ShapeDtypeStruct((columns // 2, 2 * columns), f32),
        ],
        compiler_params=pltpu.CompilerParams(vmem_limit_bytes=16 * MIB),
        name="start",
    )(x)


def shards(
    local_tiles,
    local_row,
    local_col,
    local_count,
    remote_tiles,
    remote_row,
    remote_col,
    remote_count,
    start_basis,
    start_dir,
    coeffs,
):
    size = lax.axis_size("rows")
    edge = local_tiles.shape[1]
    columns, nodes = start_basis.shape
    blocks = nodes // edge
    slots = remote_tiles.shape[1]
    node_total = nodes * size
    live = jnp.arange(slots)[None, :] < remote_count[:, None]
    packed = remote_row + blocks * jnp.where(live, remote_col, blocks)
    far_packed = lax.all_to_all(packed, "rows", split_axis=0, concat_axis=0, tiled=True).reshape(-1)
    in_tiles = lax.all_to_all(remote_tiles, "rows", split_axis=0, concat_axis=0, tiled=True)
    in_tiles = in_tiles.reshape(-1, edge, edge)
    own_tiles = remote_tiles.reshape(-1, edge, edge)
    own_dst = jnp.where(live, remote_row, blocks).reshape(-1)
    index = (remote_col.reshape(-1), own_dst, far_packed % blocks, far_packed // blocks)
    dense = dense_local(local_count, local_row, local_col, local_tiles, nodes)
    basis = start_basis
    direction = start_dir
    degree = None
    basis_bf, gram_part = start(basis)
    passes = coeffs.shape[0]
    for iteration in range(passes + 1):
        xg, inv = gather_basis(basis_bf, gram_part, size, node_total)
        out = apply_operator(iteration == 0, slots, index, dense, own_tiles, in_tiles, xg, basis, degree)
        image, cross_part = out[:2]
        if iteration == 0:
            degree = out[2]
        cross = sum_rows(cross_part, size)
        if iteration < passes:
            basis, basis_bf, direction, gram_part = update(
                False, node_total, inv, cross, image, basis, degree, coeffs[iteration], direction
            )
    return update(True, node_total, inv, cross, image, basis, degree)


def solution(mesh):
    placed = (
        P(("groups", "rows"), None, None),
        P(("groups", "rows")),
        P(("groups", "rows")),
        P(("groups", "rows")),
        P(("groups", "rows"), None, None, None),
        P(("groups", "rows"), None),
        P(("groups", "rows"), None),
        P(("groups", "rows")),
        P("groups", "rows"),
        P("groups", "rows"),
        P("groups", None, None),
    )
    return jax.shard_map(
        shards,
        mesh=mesh,
        in_specs=placed,
        out_specs=(P("groups", "rows"), P("groups", "rows"), P("groups", None)),
        check_vma=False,
    )
```

```python
import functools

import jax
import jax.numpy as jnp
from jax import lax
from jax.experimental import pallas as pl
from jax.experimental.pallas import tpu as pltpu
from jax.sharding import PartitionSpec as P

highest = lax.Precision.HIGHEST
f32 = jnp.float32
bf16 = jnp.bfloat16
NT = (((1,), (1,)), ((), ()))
MIB = 1024 * 1024


def dot_nt(a, b, precision=None):
    return lax.dot_general(a, b, NT, precision=precision, preferred_element_type=f32)


def dot_nn(a, b, precision=None):
    return jnp.dot(a, b, precision=precision, preferred_element_type=f32)


def fold(square):
    half = square.shape[0] // 2
    return jnp.concatenate([square[:half], square[half:]], axis=1)


def unfold(folded):
    half = folded.shape[1] // 2
    return jnp.concatenate([folded[:, :half], folded[:, half:]], axis=0)


def peer_barrier(targets):
    barrier = pltpu.get_barrier_semaphore()
    for target in targets:
        pl.semaphore_signal(barrier, inc=1, device_id={"rows": target}, device_id_type=pl.DeviceIdType.MESH)
    pl.semaphore_wait(barrier, len(targets))


def plane_peers(me):
    base = me - lax.rem(me, 4)
    return [base + lax.rem(me + k, 4) for k in range(1, 4)]


def line_peers(me, size):
    return [lax.rem(me + 4 * k, size) for k in range(1, size // 4)]


def send_parts(part_ref, buf, send, recv, targets):
    copies = []
    for k, target in enumerate(targets):
        copy = remote(part_ref, buf.at[k + 1], send.at[k], recv.at[k], target)
        copy.start()
        copies.append(copy)
    return copies


def ordered_sum(place, count, part_ref, buf):
    buf[0] = part_ref[...]
    total = buf[place]
    for p in range(1, count):
        total = total + buf[lax.rem(place - p + count, count)]
    return total


def remote(src, dst, send, recv, target):
    return pltpu.make_async_remote_copy(
        src_ref=src,
        dst_ref=dst,
        send_sem=send,
        recv_sem=recv,
        device_id={"rows": target},
        device_id_type=pl.DeviceIdType.MESH,
    )


def dense_kernel(per_step, count_ref, row_ref, col_ref, tiles_ref, dense_ref, acc):
    step = pl.program_id(0)
    edge = tiles_ref.shape[1]

    @pl.when(step == 0)
    def _():
        acc[...] = jnp.zeros_like(acc)

    for t in range(per_step):
        slot = step * per_step + t

        @pl.when(slot < count_ref[0])
        def _():
            r = pl.multiple_of(row_ref[slot] * edge, edge)
            c = pl.multiple_of(col_ref[slot] * edge, edge)
            acc[pl.ds(r, edge), pl.ds(c, edge)] += tiles_ref[t].astype(f32)

    @pl.when(step == pl.num_programs(0) - 1)
    def _():
        dense_ref[...] = acc[...].astype(bf16)


def dense_local(count, row, col, tiles, nodes):
    slots, edge, _ = tiles.shape
    per_step = 16
    return pl.pallas_call(
        functools.partial(dense_kernel, per_step),
        grid_spec=pltpu.PrefetchScalarGridSpec(
            num_scalar_prefetch=3,
            grid=(slots // per_step,),
            in_specs=[pl.BlockSpec((per_step, edge, edge), lambda i, *_: (i, 0, 0))],
            out_specs=pl.BlockSpec((nodes, nodes), lambda i, *_: (0, 0)),
            scratch_shapes=[pltpu.VMEM((nodes, nodes), f32)],
        ),
        out_shape=jax.ShapeDtypeStruct((nodes, nodes), bf16),
        compiler_params=pltpu.CompilerParams(vmem_limit_bytes=44 * MIB),
        cost_estimate=pl.CostEstimate(flops=10**9, bytes_accessed=40 * MIB, transcendentals=0),
        name="dense_local",
    )(count, row, col, tiles)


def back_substitute(n, first, last, both):
    rows = lax.broadcasted_iota(jnp.int32, (n, 2 * n), 0)
    lanes = lax.broadcasted_iota(jnp.int32, (n, 2 * n), 1)

    def eliminate(k, both):
        row = jnp.sum(jnp.where(rows == k, both, 0.0), axis=0, keepdims=True)
        col = jnp.sum(jnp.where(lanes == k + n, both, 0.0), axis=1, keepdims=True)
        pivot = jnp.sum(jnp.where(lanes[:1] == k + n, row, 0.0), axis=1, keepdims=True)
        scaled = row * (1.0 / pivot)
        return both - jnp.where(rows > k, col * scaled, 0.0)

    return lax.fori_loop(first, last, eliminate, both)


def gather_kernel(size, node_total, x_ref, gram_ref, xg_ref, inv_ref, plane_buf, line_buf, half_sum, p_send, p_recv,
                  l_send, l_recv, own_sem, z_send, z_recv, y_send, y_recv, s_send, s_recv):
    me = lax.axis_index("rows")
    deep = size // 4
    z = me // 4
    core = lax.rem(me, 2)
    mid = lax.rem(me // 2, 2)
    sib = me + 1 - 2 * core
    ynb = me + 2 - 4 * mid
    other = sib + 2 - 4 * mid
    up, down = lax.rem(me + 4, size), lax.rem(me - 4 + size, size)
    pieces = 2
    piece = x_ref.shape[0] // pieces

    def part(block, h):
        return xg_ref.at[block, pl.ds(h * piece, piece)]

    def along(base, k):
        return lax.rem(base + 4 * k + size, size)

    planes, lines = plane_peers(me), line_peers(me, size)
    peer_barrier(planes + lines)
    plane_copies = send_parts(gram_ref, plane_buf, p_send, p_recv, planes)

    def hop(way, k, h):
        return z_recv.at[way, k, h]

    sends = []

    def send(cond, copy):
        if cond is None:
            copy.start()
        else:
            pl.when(cond)(copy.start)
        sends.append((cond, copy))

    for h in range(pieces):
        src = x_ref.at[pl.ds(h * piece, piece)]
        send(None, remote(src, part(me, h), y_send.at[z, h], y_recv.at[z, h], ynb))
        send(z + 1 < deep, remote(src, part(me, h), z_send.at[0, 0, h], hop(0, 1, h), up))
        send(z > 0, remote(src, part(me, h), z_send.at[1, 0, h], hop(1, 1, h), down))
        send(None, remote(src, part(me, h), s_send.at[0, z, h], s_recv.at[0, z, h], sib))
    own = pltpu.make_async_copy(x_ref, xg_ref.at[me], own_sem)
    own.start()

    for copy in plane_copies:
        copy.wait()
    half_sum[...] = ordered_sum(lax.rem(me, 4), 4, gram_ref, plane_buf)
    line_copies = send_parts(half_sum, line_buf, l_send, l_recv, lines)

    def take_along_z(k):
        for h in range(pieces):
            for way, there, more, onto in (
                (0, z >= k, z + 1 < deep, up),
                (1, z + k < deep, z > 0, down),
            ):
                offset = -k if way == 0 else k
                block = along(me, offset)
                at = lax.rem(z + offset + deep, deep)
                got = part(block, h)
                pl.when(there)(remote(got, got, z_send.at[way, k, h], hop(way, k, h), onto).wait_recv)
                send(there, remote(got, got, y_send.at[at, h], y_recv.at[at, h], ynb))
                if k + 1 < deep:
                    send(
                        there & more,
                        remote(got, got, z_send.at[way, k, h], hop(way, k + 1, h), onto),
                    )
                send(there, remote(got, got, s_send.at[0, at, h], s_recv.at[0, at, h], sib))

    def take_along_y(k):
        for h in range(pieces):
            for offset, there in ((0, None),) if k == 0 else ((-k, z >= k), (k, z + k < deep)):
                block = along(ynb, offset)
                at = lax.rem(z + offset + deep, deep)
                got = part(block, h)
                wait = remote(got, got, y_send.at[at, h], y_recv.at[at, h], ynb).wait_recv
                if there is None:
                    wait()
                else:
                    pl.when(there)(wait)
                send(there, remote(got, got, s_send.at[1, at, h], s_recv.at[1, at, h], sib))

    n = inv_ref.shape[0]
    rows = lax.broadcasted_iota(jnp.int32, (n, 2 * n), 0)
    lanes = lax.broadcasted_iota(jnp.int32, (n, 2 * n), 1)
    take_along_z(1)
    for copy in line_copies:
        copy.wait()
    gram = unfold(ordered_sum(z, deep, half_sum, line_buf)) / node_total
    unit = jnp.where(rows == lanes, 1.0, 0.0)
    both = jnp.where(lanes < n, unit, jnp.concatenate([gram, gram], axis=1))
    cut = [n * k // deep for k in range(deep + 1)]
    for k in range(1, deep):
        both = back_substitute(n, cut[k - 1], cut[k], both)
        take_along_y(k - 1)
        if k + 1 < deep:
            take_along_z(k + 1)
    both = back_substitute(n, cut[deep - 1], cut[deep], both)
    take_along_y(deep - 1)
    diag = jnp.sum(jnp.where(lanes == rows + n, both, 0.0), axis=1, keepdims=True)
    inv_ref[...] = (both * (1.0 / jnp.sqrt(diag)))[:, :n]

    for at in range(deep):
        for h in range(pieces):
            for line, base in ((0, sib), (1, other)):
                got = part(lax.rem(base, 4) + 4 * at, h)
                remote(got, got, s_send.at[line, at, h], s_recv.at[line, at, h], sib).wait_recv()
    for cond, copy in sends:
        if cond is None:
            copy.wait_send()
        else:
            pl.when(cond)(copy.wait_send)
    own.wait()


def gather_basis(x_bf, gram_part, size, node_total):
    columns, nodes = x_bf.shape
    deep = size // 4
    dma = pltpu.SemaphoreType.DMA
    return pl.pallas_call(
        functools.partial(gather_kernel, size, float(node_total)),
        in_specs=[pl.BlockSpec(memory_space=pl.ANY), pl.BlockSpec(memory_space=pltpu.VMEM)],
        out_specs=[pl.BlockSpec(memory_space=pl.ANY), pl.BlockSpec(memory_space=pltpu.VMEM)],
        out_shape=[
            jax.ShapeDtypeStruct((size, columns, nodes), bf16),
            jax.ShapeDtypeStruct((columns, columns), f32),
        ],
        scratch_shapes=[
            pltpu.VMEM((4,) + gram_part.shape, f32),
            pltpu.VMEM((deep,) + gram_part.shape, f32),
            pltpu.VMEM(gram_part.shape, f32),
            dma((4,)),
            dma((4,)),
            dma((deep,)),
            dma((deep,)),
            dma,
            dma((2, deep, 2)),
            dma((2, deep, 2)),
            dma((deep, 2)),
            dma((deep, 2)),
            dma((2, deep, 2)),
            dma((2, deep, 2)),
        ],
        compiler_params=pltpu.CompilerParams(
            collective_id=0, has_side_effects=True, vmem_limit_bytes=16 * MIB
        ),
        name="gather_basis",
    )(x_bf, gram_part)


def sum_kernel(size, part_ref, out_ref, plane_buf, line_buf, half_sum, p_send, p_recv, l_send, l_recv):
    me = lax.axis_index("rows")
    planes, lines = plane_peers(me), line_peers(me, size)
    peer_barrier(planes + lines)
    for copy in send_parts(part_ref, plane_buf, p_send, p_recv, planes):
        copy.wait()
    half_sum[...] = ordered_sum(lax.rem(me, 4), 4, part_ref, plane_buf)
    for copy in send_parts(half_sum, line_buf, l_send, l_recv, lines):
        copy.wait()
    out_ref[...] = ordered_sum(me // 4, size // 4, half_sum, line_buf)


def sum_rows(part, size):
    dma = pltpu.SemaphoreType.DMA
    deep = size // 4
    return pl.pallas_call(
        functools.partial(sum_kernel, size),
        in_specs=[pl.BlockSpec(memory_space=pltpu.VMEM)],
        out_specs=pl.BlockSpec(memory_space=pltpu.VMEM),
        out_shape=jax.ShapeDtypeStruct(part.shape, f32),
        scratch_shapes=[
            pltpu.VMEM((4,) + part.shape, f32),
            pltpu.VMEM((deep,) + part.shape, f32),
            pltpu.VMEM(part.shape, f32),
            dma((4,)),
            dma((4,)),
            dma((deep,)),
            dma((deep,)),
        ],
        compiler_params=pltpu.CompilerParams(
            collective_id=1, has_side_effects=True, vmem_limit_bytes=16 * MIB
        ),
        name="sum_rows",
    )(part)


def apply_kernel(first, slots, own_src, own_dst, in_src, in_dst, *refs):
    if first:
        dense_ref, own_ref, in_ref, xg_ref, x_ref, image_ref, cross_ref, degree_ref, acc, far = refs
    else:
        dense_ref, own_ref, in_ref, xg_ref, x_ref, degree_ref, image_ref, cross_ref, acc, far = refs
    step = pl.program_id(0)
    columns, nodes = x_ref.shape
    edge = own_ref.shape[1]
    chunk = dense_ref.shape[0]

    def with_ones(x):
        if first:
            return jnp.concatenate([x, jnp.ones((16, x.shape[1]), bf16)], axis=0)
        return x

    @pl.when(step == 0)
    def _():
        acc[...] = jnp.zeros_like(acc)
        far[...] = jnp.zeros_like(far)

    x_all = with_ones(x_ref[...].astype(bf16))
    here = pl.ds(pl.multiple_of(step * chunk, chunk), chunk)
    x_here = with_ones(x_ref[:, here].astype(bf16))
    dense = dense_ref[...]
    acc[...] += dot_nn(x_here, dense)
    acc[:, here] += dot_nt(x_all, dense)

    count = own_ref.shape[0]
    blocks = nodes // edge
    for tiles_ref, src_ref, dst_ref, dot in (
        (own_ref, own_src, own_dst, dot_nt),
        (in_ref, in_src, in_dst, dot_nn),
    ):
        products = []
        for t in range(count):
            slot = step * count + t
            at = pl.ds(pl.multiple_of(src_ref[slot] * edge, edge), edge)
            if dot is dot_nt:
                tile = tiles_ref[t]
            else:
                tile = tiles_ref[t // slots, (t % slots) * edge : (t % slots + 1) * edge]
            products.append(dot(with_ones(xg_ref[slot // slots, :, at]), tile))
        for t in range(count):
            far[dst_ref[step * count + t]] += products[t]

    @pl.when(step == pl.num_programs(0) - 1)
    def _():
        for b in range(blocks):
            at = slice(b * edge, (b + 1) * edge)
            both = acc[:, at] + far[b]
            if first:
                degree = 0.5 * both[columns : columns + 1]
                degree_ref[:, at] = jnp.broadcast_to(degree, (8, edge))
            else:
                degree = degree_ref[:1, at]
            image_ref[:, at] = degree * x_ref[:, at] - 0.5 * both[:columns]
        cross_ref[...] = fold(dot_nt(image_ref[...], x_ref[...], highest))


def apply_operator(first, slots, index, dense, own_tiles, in_tiles, xg, x, degree):
    columns, nodes = x.shape
    edge = own_tiles.shape[1]
    steps = 8
    chunk = nodes // steps
    count = own_tiles.shape[0] // steps
    whole = lambda shape: pl.BlockSpec(shape, lambda i, *_: (0,) * len(shape))
    rows = columns + 16 if first else columns
    tile_spec = pl.BlockSpec((count, edge, edge), lambda i, *_: (i, 0, 0))
    degree_shape = (8, nodes)
    in_specs = [
        pl.BlockSpec((chunk, nodes), lambda i, *_: (i, 0)),
        tile_spec,
        pl.BlockSpec((count // slots,) + in_tiles.shape[1:], lambda i, *_: (i, 0, 0)),
        whole(xg.shape),
        whole(x.shape),
    ]
    out_specs = [whole(x.shape), whole((columns // 2, 2 * columns))]
    out_shape = [
        jax.ShapeDtypeStruct(x.shape, f32),
        jax.ShapeDtypeStruct((columns // 2, 2 * columns), f32),
    ]
    operands = [dense, own_tiles, in_tiles, xg, x]
    if first:
        out_specs.append(whole(degree_shape))
        out_shape.append(jax.ShapeDtypeStruct(degree_shape, f32))
    else:
        in_specs.append(whole(degree_shape))
        operands.append(degree)
    return pl.pallas_call(
        functools.partial(apply_kernel, first, slots),
        grid_spec=pltpu.PrefetchScalarGridSpec(
            num_scalar_prefetch=4,
            grid=(steps,),
            in_specs=in_specs,
            out_specs=out_specs,
            scratch_shapes=[
                pltpu.VMEM((rows, nodes), f32),
                pltpu.VMEM((nodes // edge + 1, rows, edge), f32),
            ],
        ),
        out_shape=out_shape,
        compiler_params=pltpu.CompilerParams(vmem_limit_bytes=44 * MIB),
        name="apply_operator",
    )(*index, *operands)


def update_kernel(last, node_total, inv_ref, cross_ref, image_ref, x_ref, degree_ref, *refs):
    inv = inv_ref[...]
    n = inv.shape[0]
    cross = unfold(cross_ref[...]) / node_total
    projected = dot_nt(dot_nn(inv, cross, highest), inv, highest)
    scale = 1.0 / (1.0 + degree_ref[:1, :])
    x = x_ref[...]
    p_inv = dot_nn(projected, inv, highest)
    if last:
        ortho_ref, residual_ref, projected_ref = refs
        ortho_ref[...] = dot_nn(inv, x, highest)
        residual_ref[...] = (dot_nn(inv, image_ref[...], highest) - dot_nn(p_inv, x, highest)) * scale
        projected_ref[...] = projected
    else:
        coeff_ref, dir_ref, x_out, bf_out, dir_out, gram_out = refs
        c_x, c_r, c_p = coeff_ref[:, :n], coeff_ref[:, n : 2 * n], coeff_ref[:, 2 * n :]
        m_image = dot_nn(c_r, inv, highest)
        m_x = dot_nn(c_r, p_inv, highest)
        m_basis = dot_nn(c_x, inv, highest)
        direction = (dot_nn(m_image, image_ref[...], highest) - dot_nn(m_x, x, highest)) * scale
        direction = direction + dot_nn(c_p, dir_ref[...], highest)
        basis = dot_nn(m_basis, x, highest) + direction
        dir_out[...] = direction
        x_out[...] = basis
        bf_out[...] = basis.astype(bf16)
        gram_out[...] = fold(dot_nt(basis, basis, highest))


def update(last, node_total, inv, cross, image, x, degree, coeff=None, direction=None):
    columns, nodes = x.shape
    big = jax.ShapeDtypeStruct((columns, nodes), f32)
    if last:
        shapes = [big, big, jax.ShapeDtypeStruct((columns, columns), f32)]
        operands = (inv, cross, image, x, degree)
    else:
        shapes = [
            big,
            jax.ShapeDtypeStruct((columns, nodes), bf16),
            big,
            jax.ShapeDtypeStruct((columns // 2, 2 * columns), f32),
        ]
        operands = (inv, cross, image, x, degree, coeff, direction)
    vmem = pl.BlockSpec(memory_space=pltpu.VMEM)
    return pl.pallas_call(
        functools.partial(update_kernel, last, float(node_total)),
        in_specs=[vmem] * len(operands),
        out_specs=[vmem] * len(shapes),
        out_shape=shapes,
        compiler_params=pltpu.CompilerParams(vmem_limit_bytes=32 * MIB),
        name="update",
    )(*operands)


def start_kernel(x_ref, bf_out, gram_out):
    x = x_ref[...]
    bf_out[...] = x.astype(bf16)
    gram_out[...] = fold(dot_nt(x, x, highest))


def start(x):
    columns, nodes = x.shape
    vmem = pl.BlockSpec(memory_space=pltpu.VMEM)
    return pl.pallas_call(
        start_kernel,
        in_specs=[vmem],
        out_specs=[vmem] * 2,
        out_shape=[
            jax.ShapeDtypeStruct((columns, nodes), bf16),
            jax.ShapeDtypeStruct((columns // 2, 2 * columns), f32),
        ],
        compiler_params=pltpu.CompilerParams(vmem_limit_bytes=16 * MIB),
        name="start",
    )(x)


def shards(
    local_tiles,
    local_row,
    local_col,
    local_count,
    remote_tiles,
    remote_row,
    remote_col,
    remote_count,
    start_basis,
    start_dir,
    coeffs,
):
    size = lax.axis_size("rows")
    edge = local_tiles.shape[1]
    columns, nodes = start_basis.shape
    blocks = nodes // edge
    slots = remote_tiles.shape[1]
    node_total = nodes * size
    live = jnp.arange(slots)[None, :] < remote_count[:, None]
    numbers = jnp.concatenate([remote_row, jnp.where(live, remote_col, blocks)], axis=1).astype(bf16)
    numbers = jnp.pad(numbers[:, None, :], ((0, 0), (0, 15), (0, edge - 2 * slots)))
    slab = jnp.concatenate([remote_tiles.reshape(size, slots * edge, edge), numbers], axis=1)
    in_tiles = lax.all_to_all(slab, "rows", split_axis=0, concat_axis=0, tiled=True)
    far = in_tiles[:, slots * edge, : 2 * slots].astype(jnp.int32)
    own_tiles = remote_tiles.reshape(-1, edge, edge)
    own_dst = jnp.where(live, remote_row, blocks).reshape(-1)
    index = (
        remote_col.reshape(-1),
        own_dst,
        far[:, :slots].reshape(-1),
        far[:, slots:].reshape(-1),
    )
    dense = dense_local(local_count, local_row, local_col, local_tiles, nodes)
    basis = start_basis
    direction = start_dir
    degree = None
    basis_bf, gram_part = start(basis)
    dense, basis_bf = lax.optimization_barrier((dense, basis_bf))
    passes = coeffs.shape[0]
    for iteration in range(passes + 1):
        xg, inv = gather_basis(basis_bf, gram_part, size, node_total)
        out = apply_operator(iteration == 0, slots, index, dense, own_tiles, in_tiles, xg, basis, degree)
        image, cross_part = out[:2]
        if iteration == 0:
            degree = out[2]
        cross = sum_rows(cross_part, size)
        if iteration < passes:
            basis, basis_bf, direction, gram_part = update(
                False, node_total, inv, cross, image, basis, degree, coeffs[iteration], direction
            )
    return update(True, node_total, inv, cross, image, basis, degree)


def solution(mesh):
    placed = (
        P(("groups", "rows"), None, None),
        P(("groups", "rows")),
        P(("groups", "rows")),
        P(("groups", "rows")),
        P(("groups", "rows"), None, None, None),
        P(("groups", "rows"), None),
        P(("groups", "rows"), None),
        P(("groups", "rows")),
        P("groups", "rows"),
        P("groups", "rows"),
        P("groups", None, None),
    )
    return jax.shard_map(
        shards,
        mesh=mesh,
        in_specs=placed,
        out_specs=(P("groups", "rows"), P("groups", "rows"), P("groups", None)),
        check_vma=False,
    )
```

```python
import functools

import jax
import jax.numpy as jnp
from jax import lax
from jax.experimental import pallas as pl
from jax.experimental.pallas import tpu as pltpu
from jax.sharding import PartitionSpec as P

highest = lax.Precision.HIGHEST
f32 = jnp.float32
bf16 = jnp.bfloat16
NT = (((1,), (1,)), ((), ()))
MIB = 1024 * 1024


def dot_nt(a, b, precision=None):
    return lax.dot_general(a, b, NT, precision=precision, preferred_element_type=f32)


def dot_nn(a, b, precision=None):
    return jnp.dot(a, b, precision=precision, preferred_element_type=f32)


def fold(square):
    half = square.shape[0] // 2
    return jnp.concatenate([square[:half], square[half:]], axis=1)


def unfold(folded):
    half = folded.shape[1] // 2
    return jnp.concatenate([folded[:, :half], folded[:, half:]], axis=0)


def peer_barrier(targets):
    barrier = pltpu.get_barrier_semaphore()
    for target in targets:
        pl.semaphore_signal(barrier, inc=1, device_id={"rows": target}, device_id_type=pl.DeviceIdType.MESH)
    pl.semaphore_wait(barrier, len(targets))


def plane_peers(me):
    base = me - lax.rem(me, 4)
    return [base + lax.rem(me + k, 4) for k in range(1, 4)]


def line_peers(me, size):
    return [lax.rem(me + 4 * k, size) for k in range(1, size // 4)]


def send_parts(part_ref, buf, send, recv, targets):
    copies = []
    for k, target in enumerate(targets):
        copy = remote(part_ref, buf.at[k + 1], send.at[k], recv.at[k], target)
        copy.start()
        copies.append(copy)
    return copies


def ordered_sum(place, count, part_ref, buf):
    buf[0] = part_ref[...]
    total = buf[place]
    for p in range(1, count):
        total = total + buf[lax.rem(place - p + count, count)]
    return total


def remote(src, dst, send, recv, target):
    return pltpu.make_async_remote_copy(
        src_ref=src,
        dst_ref=dst,
        send_sem=send,
        recv_sem=recv,
        device_id={"rows": target},
        device_id_type=pl.DeviceIdType.MESH,
    )


def dense_kernel(per_step, count_ref, row_ref, col_ref, tiles_ref, dense_ref, acc):
    step = pl.program_id(0)
    edge = tiles_ref.shape[1]

    @pl.when(step == 0)
    def _():
        acc[...] = jnp.zeros_like(acc)

    for t in range(per_step):
        slot = step * per_step + t

        @pl.when(slot < count_ref[0])
        def _():
            r = pl.multiple_of(row_ref[slot] * edge, edge)
            c = pl.multiple_of(col_ref[slot] * edge, edge)
            acc[pl.ds(r, edge), pl.ds(c, edge)] += tiles_ref[t].astype(f32)

    @pl.when(step == pl.num_programs(0) - 1)
    def _():
        dense_ref[...] = acc[...].astype(bf16)


def dense_local(count, row, col, tiles, nodes):
    slots, edge, _ = tiles.shape
    per_step = 16
    return pl.pallas_call(
        functools.partial(dense_kernel, per_step),
        grid_spec=pltpu.PrefetchScalarGridSpec(
            num_scalar_prefetch=3,
            grid=(slots // per_step,),
            in_specs=[pl.BlockSpec((per_step, edge, edge), lambda i, *_: (i, 0, 0))],
            out_specs=pl.BlockSpec((nodes, nodes), lambda i, *_: (0, 0)),
            scratch_shapes=[pltpu.VMEM((nodes, nodes), f32)],
        ),
        out_shape=jax.ShapeDtypeStruct((nodes, nodes), bf16),
        compiler_params=pltpu.CompilerParams(vmem_limit_bytes=44 * MIB),
        cost_estimate=pl.CostEstimate(flops=10**9, bytes_accessed=40 * MIB, transcendentals=0),
        name="dense_local",
    )(count, row, col, tiles)


def back_substitute(n, first, last, both):
    rows = lax.broadcasted_iota(jnp.int32, (n, 2 * n), 0)
    lanes = lax.broadcasted_iota(jnp.int32, (n, 2 * n), 1)

    def eliminate(k, both):
        row = jnp.sum(jnp.where(rows == k, both, 0.0), axis=0, keepdims=True)
        col = jnp.sum(jnp.where(lanes == k + n, both, 0.0), axis=1, keepdims=True)
        pivot = jnp.sum(jnp.where(lanes[:1] == k + n, row, 0.0), axis=1, keepdims=True)
        scaled = row * (1.0 / pivot)
        return both - jnp.where(rows > k, col * scaled, 0.0)

    return lax.fori_loop(first, last, eliminate, both)


def gather_kernel(size, node_total, x_ref, gram_ref, dense_ref, xg_ref, inv_ref, local_ref, plane_buf, line_buf, half_sum, p_send, p_recv,
                  l_send, l_recv, own_sem, z_send, z_recv, y_send, y_recv, s_send, s_recv):
    me = lax.axis_index("rows")
    deep = size // 4
    z = me // 4
    core = lax.rem(me, 2)
    mid = lax.rem(me // 2, 2)
    sib = me + 1 - 2 * core
    ynb = me + 2 - 4 * mid
    other = sib + 2 - 4 * mid
    up, down = lax.rem(me + 4, size), lax.rem(me - 4 + size, size)
    pieces = 2
    piece = x_ref.shape[0] // pieces

    def part(block, h):
        return xg_ref.at[block, pl.ds(h * piece, piece)]

    def along(base, k):
        return lax.rem(base + 4 * k + size, size)

    columns, nodes = x_ref.shape
    ones = jnp.ones((local_ref.shape[0] - columns, nodes), bf16)
    x_all = jnp.concatenate([x_ref[...], ones], axis=0)
    turns = 2 * deep
    chunk = nodes // turns

    def local_turns(first, last):
        def turn(i, nothing):
            here = pl.ds(pl.multiple_of(i * chunk, chunk), chunk)
            x_here = jnp.concatenate([x_ref[:, here], ones[:, :chunk]], axis=0)
            local_ref[...] += dot_nn(x_here, dense_ref[here, :])
            local_ref[:, here] += dot_nt(x_all, dense_ref[here, :])
            return nothing

        lax.fori_loop(first, last, turn, 0)

    planes, lines = plane_peers(me), line_peers(me, size)
    peer_barrier(planes + lines)
    plane_copies = send_parts(gram_ref, plane_buf, p_send, p_recv, planes)

    def hop(way, k, h):
        return z_recv.at[way, k, h]

    sends = []

    def send(cond, copy):
        if cond is None:
            copy.start()
        else:
            pl.when(cond)(copy.start)
        sends.append((cond, copy))

    for h in range(pieces):
        src = x_ref.at[pl.ds(h * piece, piece)]
        send(None, remote(src, part(me, h), y_send.at[z, h], y_recv.at[z, h], ynb))
        send(z + 1 < deep, remote(src, part(me, h), z_send.at[0, 0, h], hop(0, 1, h), up))
        send(z > 0, remote(src, part(me, h), z_send.at[1, 0, h], hop(1, 1, h), down))
        send(None, remote(src, part(me, h), s_send.at[0, z, h], s_recv.at[0, z, h], sib))
    own = pltpu.make_async_copy(x_ref, xg_ref.at[me], own_sem)
    own.start()
    local_ref[...] = jnp.zeros_like(local_ref)

    for copy in plane_copies:
        copy.wait()
    half_sum[...] = ordered_sum(lax.rem(me, 4), 4, gram_ref, plane_buf)
    line_copies = send_parts(half_sum, line_buf, l_send, l_recv, lines)

    def take_along_z(k):
        for h in range(pieces):
            for way, there, more, onto in (
                (0, z >= k, z + 1 < deep, up),
                (1, z + k < deep, z > 0, down),
            ):
                offset = -k if way == 0 else k
                block = along(me, offset)
                at = lax.rem(z + offset + deep, deep)
                got = part(block, h)
                pl.when(there)(remote(got, got, z_send.at[way, k, h], hop(way, k, h), onto).wait_recv)
                send(there, remote(got, got, y_send.at[at, h], y_recv.at[at, h], ynb))
                if k + 1 < deep:
                    send(
                        there & more,
                        remote(got, got, z_send.at[way, k, h], hop(way, k + 1, h), onto),
                    )
                send(there, remote(got, got, s_send.at[0, at, h], s_recv.at[0, at, h], sib))

    def take_along_y(k):
        for h in range(pieces):
            for offset, there in ((0, None),) if k == 0 else ((-k, z >= k), (k, z + k < deep)):
                block = along(ynb, offset)
                at = lax.rem(z + offset + deep, deep)
                got = part(block, h)
                wait = remote(got, got, y_send.at[at, h], y_recv.at[at, h], ynb).wait_recv
                if there is None:
                    wait()
                else:
                    pl.when(there)(wait)
                send(there, remote(got, got, s_send.at[1, at, h], s_recv.at[1, at, h], sib))

    n = inv_ref.shape[0]
    rows = lax.broadcasted_iota(jnp.int32, (n, 2 * n), 0)
    lanes = lax.broadcasted_iota(jnp.int32, (n, 2 * n), 1)
    local_turns(0, 2)
    take_along_z(1)
    for copy in line_copies:
        copy.wait()
    gram = unfold(ordered_sum(z, deep, half_sum, line_buf)) / node_total
    unit = jnp.where(rows == lanes, 1.0, 0.0)
    both = jnp.where(lanes < n, unit, jnp.concatenate([gram, gram], axis=1))
    cut = [n * k // deep for k in range(deep + 1)]
    for k in range(1, deep):
        both = back_substitute(n, cut[k - 1], cut[k], both)
        take_along_y(k - 1)
        local_turns(2 * k, 2 * k + 2)
        if k + 1 < deep:
            take_along_z(k + 1)
    both = back_substitute(n, cut[deep - 1], cut[deep], both)
    take_along_y(deep - 1)
    diag = jnp.sum(jnp.where(lanes == rows + n, both, 0.0), axis=1, keepdims=True)
    inv_ref[...] = (both * (1.0 / jnp.sqrt(diag)))[:, :n]

    for at in range(deep):
        for h in range(pieces):
            for line, base in ((0, sib), (1, other)):
                got = part(lax.rem(base, 4) + 4 * at, h)
                remote(got, got, s_send.at[line, at, h], s_recv.at[line, at, h], sib).wait_recv()
    for cond, copy in sends:
        if cond is None:
            copy.wait_send()
        else:
            pl.when(cond)(copy.wait_send)
    own.wait()


def gather_basis(x_bf, gram_part, dense, size, node_total):
    columns, nodes = x_bf.shape
    deep = size // 4
    dma = pltpu.SemaphoreType.DMA
    return pl.pallas_call(
        functools.partial(gather_kernel, size, float(node_total)),
        in_specs=[pl.BlockSpec(memory_space=pltpu.VMEM)] * 3,
        out_specs=[pl.BlockSpec(memory_space=pl.ANY)] + [pl.BlockSpec(memory_space=pltpu.VMEM)] * 2,
        out_shape=[
            jax.ShapeDtypeStruct((size, columns, nodes), bf16),
            jax.ShapeDtypeStruct((columns, columns), f32),
            jax.ShapeDtypeStruct((columns + 16, nodes), f32),
        ],
        scratch_shapes=[
            pltpu.VMEM((4,) + gram_part.shape, f32),
            pltpu.VMEM((deep,) + gram_part.shape, f32),
            pltpu.VMEM(gram_part.shape, f32),
            dma((4,)),
            dma((4,)),
            dma((deep,)),
            dma((deep,)),
            dma,
            dma((2, deep, 2)),
            dma((2, deep, 2)),
            dma((deep, 2)),
            dma((deep, 2)),
            dma((2, deep, 2)),
            dma((2, deep, 2)),
        ],
        compiler_params=pltpu.CompilerParams(
            collective_id=0, has_side_effects=True, vmem_limit_bytes=20 * MIB
        ),
        name="gather_basis",
    )(x_bf, gram_part, dense)


def sum_kernel(size, part_ref, out_ref, plane_buf, line_buf, half_sum, p_send, p_recv, l_send, l_recv):
    me = lax.axis_index("rows")
    planes, lines = plane_peers(me), line_peers(me, size)
    peer_barrier(planes + lines)
    for copy in send_parts(part_ref, plane_buf, p_send, p_recv, planes):
        copy.wait()
    half_sum[...] = ordered_sum(lax.rem(me, 4), 4, part_ref, plane_buf)
    for copy in send_parts(half_sum, line_buf, l_send, l_recv, lines):
        copy.wait()
    out_ref[...] = ordered_sum(me // 4, size // 4, half_sum, line_buf)


def sum_rows(part, size):
    dma = pltpu.SemaphoreType.DMA
    deep = size // 4
    return pl.pallas_call(
        functools.partial(sum_kernel, size),
        in_specs=[pl.BlockSpec(memory_space=pltpu.VMEM)],
        out_specs=pl.BlockSpec(memory_space=pltpu.VMEM),
        out_shape=jax.ShapeDtypeStruct(part.shape, f32),
        scratch_shapes=[
            pltpu.VMEM((4,) + part.shape, f32),
            pltpu.VMEM((deep,) + part.shape, f32),
            pltpu.VMEM(part.shape, f32),
            dma((4,)),
            dma((4,)),
            dma((deep,)),
            dma((deep,)),
        ],
        compiler_params=pltpu.CompilerParams(
            collective_id=1, has_side_effects=True, vmem_limit_bytes=16 * MIB
        ),
        name="sum_rows",
    )(part)


def apply_kernel(first, slots, own_src, own_dst, in_src, in_dst, *refs):
    if first:
        local_ref, own_ref, in_ref, xg_ref, x_ref, image_ref, cross_ref, degree_ref, far = refs
    else:
        local_ref, own_ref, in_ref, xg_ref, x_ref, degree_ref, image_ref, cross_ref, far = refs
    step = pl.program_id(0)
    columns, nodes = x_ref.shape
    rows = far.shape[1]
    edge = own_ref.shape[1]

    def with_ones(x):
        if first:
            return jnp.concatenate([x, jnp.ones((16, x.shape[1]), bf16)], axis=0)
        return x

    @pl.when(step == 0)
    def _():
        far[...] = jnp.zeros_like(far)

    count = own_ref.shape[0]
    blocks = nodes // edge
    for tiles_ref, src_ref, dst_ref, dot in (
        (own_ref, own_src, own_dst, dot_nt),
        (in_ref, in_src, in_dst, dot_nn),
    ):
        products = []
        for t in range(count):
            slot = step * count + t
            at = pl.ds(pl.multiple_of(src_ref[slot] * edge, edge), edge)
            if dot is dot_nt:
                tile = tiles_ref[t]
            else:
                tile = tiles_ref[t // slots, (t % slots) * edge : (t % slots + 1) * edge]
            products.append(dot(with_ones(xg_ref[slot // slots, :, at]), tile))
        for t in range(count):
            far[dst_ref[step * count + t]] += products[t]

    @pl.when(step == pl.num_programs(0) - 1)
    def _():
        for b in range(blocks):
            at = slice(b * edge, (b + 1) * edge)
            both = local_ref[:rows, at] + far[b]
            if first:
                degree = 0.5 * both[columns : columns + 1]
                degree_ref[:, at] = jnp.broadcast_to(degree, (8, edge))
            else:
                degree = degree_ref[:1, at]
            image_ref[:, at] = degree * x_ref[:, at] - 0.5 * both[:columns]
        cross_ref[...] = fold(dot_nt(image_ref[...], x_ref[...], highest))


def apply_operator(first, slots, index, local, own_tiles, in_tiles, xg, x, degree):
    columns, nodes = x.shape
    edge = own_tiles.shape[1]
    steps = 8
    count = own_tiles.shape[0] // steps
    whole = lambda shape: pl.BlockSpec(shape, lambda i, *_: (0,) * len(shape))
    rows = columns + 16 if first else columns
    tile_spec = pl.BlockSpec((count, edge, edge), lambda i, *_: (i, 0, 0))
    degree_shape = (8, nodes)
    in_specs = [
        whole(local.shape),
        tile_spec,
        pl.BlockSpec((count // slots,) + in_tiles.shape[1:], lambda i, *_: (i, 0, 0)),
        whole(xg.shape),
        whole(x.shape),
    ]
    out_specs = [whole(x.shape), whole((columns // 2, 2 * columns))]
    out_shape = [
        jax.ShapeDtypeStruct(x.shape, f32),
        jax.ShapeDtypeStruct((columns // 2, 2 * columns), f32),
    ]
    operands = [local, own_tiles, in_tiles, xg, x]
    if first:
        out_specs.append(whole(degree_shape))
        out_shape.append(jax.ShapeDtypeStruct(degree_shape, f32))
    else:
        in_specs.append(whole(degree_shape))
        operands.append(degree)
    return pl.pallas_call(
        functools.partial(apply_kernel, first, slots),
        grid_spec=pltpu.PrefetchScalarGridSpec(
            num_scalar_prefetch=4,
            grid=(steps,),
            in_specs=in_specs,
            out_specs=out_specs,
            scratch_shapes=[
                pltpu.VMEM((nodes // edge + 1, rows, edge), f32),
            ],
        ),
        out_shape=out_shape,
        compiler_params=pltpu.CompilerParams(vmem_limit_bytes=32 * MIB),
        name="apply_operator",
    )(*index, *operands)


def update_kernel(last, node_total, inv_ref, cross_ref, image_ref, x_ref, degree_ref, *refs):
    inv = inv_ref[...]
    n = inv.shape[0]
    cross = unfold(cross_ref[...]) / node_total
    projected = dot_nt(dot_nn(inv, cross, highest), inv, highest)
    scale = 1.0 / (1.0 + degree_ref[:1, :])
    x = x_ref[...]
    p_inv = dot_nn(projected, inv, highest)
    if last:
        ortho_ref, residual_ref, projected_ref = refs
        ortho_ref[...] = dot_nn(inv, x, highest)
        residual_ref[...] = (dot_nn(inv, image_ref[...], highest) - dot_nn(p_inv, x, highest)) * scale
        projected_ref[...] = projected
    else:
        coeff_ref, dir_ref, x_out, bf_out, dir_out, gram_out = refs
        c_x, c_r, c_p = coeff_ref[:, :n], coeff_ref[:, n : 2 * n], coeff_ref[:, 2 * n :]
        m_image = dot_nn(c_r, inv, highest)
        m_x = dot_nn(c_r, p_inv, highest)
        m_basis = dot_nn(c_x, inv, highest)
        direction = (dot_nn(m_image, image_ref[...], highest) - dot_nn(m_x, x, highest)) * scale
        direction = direction + dot_nn(c_p, dir_ref[...], highest)
        basis = dot_nn(m_basis, x, highest) + direction
        dir_out[...] = direction
        x_out[...] = basis
        bf_out[...] = basis.astype(bf16)
        gram_out[...] = fold(dot_nt(basis, basis, highest))


def update(last, node_total, inv, cross, image, x, degree, coeff=None, direction=None):
    columns, nodes = x.shape
    big = jax.ShapeDtypeStruct((columns, nodes), f32)
    if last:
        shapes = [big, big, jax.ShapeDtypeStruct((columns, columns), f32)]
        operands = (inv, cross, image, x, degree)
    else:
        shapes = [
            big,
            jax.ShapeDtypeStruct((columns, nodes), bf16),
            big,
            jax.ShapeDtypeStruct((columns // 2, 2 * columns), f32),
        ]
        operands = (inv, cross, image, x, degree, coeff, direction)
    vmem = pl.BlockSpec(memory_space=pltpu.VMEM)
    return pl.pallas_call(
        functools.partial(update_kernel, last, float(node_total)),
        in_specs=[vmem] * len(operands),
        out_specs=[vmem] * len(shapes),
        out_shape=shapes,
        compiler_params=pltpu.CompilerParams(vmem_limit_bytes=32 * MIB),
        name="update",
    )(*operands)


def start_kernel(x_ref, bf_out, gram_out):
    x = x_ref[...]
    bf_out[...] = x.astype(bf16)
    gram_out[...] = fold(dot_nt(x, x, highest))


def start(x):
    columns, nodes = x.shape
    vmem = pl.BlockSpec(memory_space=pltpu.VMEM)
    return pl.pallas_call(
        start_kernel,
        in_specs=[vmem],
        out_specs=[vmem] * 2,
        out_shape=[
            jax.ShapeDtypeStruct((columns, nodes), bf16),
            jax.ShapeDtypeStruct((columns // 2, 2 * columns), f32),
        ],
        compiler_params=pltpu.CompilerParams(vmem_limit_bytes=16 * MIB),
        name="start",
    )(x)


def shards(
    local_tiles,
    local_row,
    local_col,
    local_count,
    remote_tiles,
    remote_row,
    remote_col,
    remote_count,
    start_basis,
    start_dir,
    coeffs,
):
    size = lax.axis_size("rows")
    edge = local_tiles.shape[1]
    columns, nodes = start_basis.shape
    blocks = nodes // edge
    slots = remote_tiles.shape[1]
    node_total = nodes * size
    live = jnp.arange(slots)[None, :] < remote_count[:, None]
    numbers = jnp.concatenate([remote_row, jnp.where(live, remote_col, blocks)], axis=1).astype(bf16)
    numbers = jnp.pad(numbers[:, None, :], ((0, 0), (0, 15), (0, edge - 2 * slots)))
    slab = jnp.concatenate([remote_tiles.reshape(size, slots * edge, edge), numbers], axis=1)
    in_tiles = lax.all_to_all(slab, "rows", split_axis=0, concat_axis=0, tiled=True)
    far = in_tiles[:, slots * edge, : 2 * slots].astype(jnp.int32)
    own_tiles = remote_tiles.reshape(-1, edge, edge)
    own_dst = jnp.where(live, remote_row, blocks).reshape(-1)
    index = (
        remote_col.reshape(-1),
        own_dst,
        far[:, :slots].reshape(-1),
        far[:, slots:].reshape(-1),
    )
    dense = dense_local(local_count, local_row, local_col, local_tiles, nodes)
    basis = start_basis
    direction = start_dir
    degree = None
    basis_bf, gram_part = start(basis)
    dense, basis_bf = lax.optimization_barrier((dense, basis_bf))
    passes = coeffs.shape[0]
    for iteration in range(passes + 1):
        xg, inv, local = gather_basis(basis_bf, gram_part, dense, size, node_total)
        out = apply_operator(iteration == 0, slots, index, local, own_tiles, in_tiles, xg, basis, degree)
        image, cross_part = out[:2]
        if iteration == 0:
            degree = out[2]
        cross = sum_rows(cross_part, size)
        if iteration < passes:
            basis, basis_bf, direction, gram_part = update(
                False, node_total, inv, cross, image, basis, degree, coeffs[iteration], direction
            )
    return update(True, node_total, inv, cross, image, basis, degree)


def solution(mesh):
    placed = (
        P(("groups", "rows"), None, None),
        P(("groups", "rows")),
        P(("groups", "rows")),
        P(("groups", "rows")),
        P(("groups", "rows"), None, None, None),
        P(("groups", "rows"), None),
        P(("groups", "rows"), None),
        P(("groups", "rows")),
        P("groups", "rows"),
        P("groups", "rows"),
        P("groups", None, None),
    )
    return jax.shard_map(
        shards,
        mesh=mesh,
        in_specs=placed,
        out_specs=(P("groups", "rows"), P("groups", "rows"), P("groups", None)),
        check_vma=False,
    )
```

```python
import functools

import jax
import jax.numpy as jnp
from jax import lax
from jax.experimental import pallas as pl
from jax.experimental.pallas import tpu as pltpu
from jax.sharding import PartitionSpec as P

highest = lax.Precision.HIGHEST
f32 = jnp.float32
bf16 = jnp.bfloat16
NT = (((1,), (1,)), ((), ()))
MIB = 1024 * 1024


def dot_nt(a, b, precision=None):
    return lax.dot_general(a, b, NT, precision=precision, preferred_element_type=f32)


def dot_nn(a, b, precision=None):
    return jnp.dot(a, b, precision=precision, preferred_element_type=f32)


def fold(square):
    half = square.shape[0] // 2
    return jnp.concatenate([square[:half], square[half:]], axis=1)


def unfold(folded):
    half = folded.shape[1] // 2
    return jnp.concatenate([folded[:, :half], folded[:, half:]], axis=0)


def peer_barrier(targets):
    barrier = pltpu.get_barrier_semaphore()
    for target in targets:
        pl.semaphore_signal(barrier, inc=1, device_id={"rows": target}, device_id_type=pl.DeviceIdType.MESH)
    pl.semaphore_wait(barrier, len(targets))


def plane_peers(me):
    base = me - lax.rem(me, 4)
    return [base + lax.rem(me + k, 4) for k in range(1, 4)]


def line_peers(me, size):
    return [lax.rem(me + 4 * k, size) for k in range(1, size // 4)]


def send_parts(part_ref, buf, send, recv, targets):
    copies = []
    for k, target in enumerate(targets):
        copy = remote(part_ref, buf.at[k + 1], send.at[k], recv.at[k], target)
        copy.start()
        copies.append(copy)
    return copies


def ordered_sum(place, count, part_ref, buf):
    buf[0] = part_ref[...]
    total = buf[place]
    for p in range(1, count):
        total = total + buf[lax.rem(place - p + count, count)]
    return total


def remote(src, dst, send, recv, target):
    return pltpu.make_async_remote_copy(
        src_ref=src,
        dst_ref=dst,
        send_sem=send,
        recv_sem=recv,
        device_id={"rows": target},
        device_id_type=pl.DeviceIdType.MESH,
    )


def dense_kernel(per_step, count_ref, row_ref, col_ref, tiles_ref, dense_ref, acc):
    step = pl.program_id(0)
    edge = tiles_ref.shape[1]

    @pl.when(step == 0)
    def _():
        acc[...] = jnp.zeros_like(acc)

    for t in range(per_step):
        slot = step * per_step + t

        @pl.when(slot < count_ref[0])
        def _():
            r = pl.multiple_of(row_ref[slot] * edge, edge)
            c = pl.multiple_of(col_ref[slot] * edge, edge)
            acc[pl.ds(r, edge), pl.ds(c, edge)] += tiles_ref[t].astype(f32)

    @pl.when(step == pl.num_programs(0) - 1)
    def _():
        dense_ref[...] = acc[...].astype(bf16)


def dense_local(count, row, col, tiles, nodes):
    slots, edge, _ = tiles.shape
    per_step = 16
    return pl.pallas_call(
        functools.partial(dense_kernel, per_step),
        grid_spec=pltpu.PrefetchScalarGridSpec(
            num_scalar_prefetch=3,
            grid=(slots // per_step,),
            in_specs=[pl.BlockSpec((per_step, edge, edge), lambda i, *_: (i, 0, 0))],
            out_specs=pl.BlockSpec((nodes, nodes), lambda i, *_: (0, 0)),
            scratch_shapes=[pltpu.VMEM((nodes, nodes), f32)],
        ),
        out_shape=jax.ShapeDtypeStruct((nodes, nodes), bf16),
        compiler_params=pltpu.CompilerParams(vmem_limit_bytes=44 * MIB),
        cost_estimate=pl.CostEstimate(flops=10**9, bytes_accessed=40 * MIB, transcendentals=0),
        name="dense_local",
    )(count, row, col, tiles)


def back_substitute(n, first, last, both):
    rows = lax.broadcasted_iota(jnp.int32, (n, 2 * n), 0)
    lanes = lax.broadcasted_iota(jnp.int32, (n, 2 * n), 1)

    def eliminate(k, both):
        row = jnp.sum(jnp.where(rows == k, both, 0.0), axis=0, keepdims=True)
        col = jnp.sum(jnp.where(lanes == k + n, both, 0.0), axis=1, keepdims=True)
        pivot = jnp.sum(jnp.where(lanes[:1] == k + n, row, 0.0), axis=1, keepdims=True)
        scaled = row * (1.0 / pivot)
        return both - jnp.where(rows > k, col * scaled, 0.0)

    return lax.fori_loop(first, last, eliminate, both)


def gather_kernel(size, node_total, x_ref, gram_ref, dense_ref, xg_ref, inv_ref, local_ref, plane_buf, line_buf, half_sum, p_send, p_recv,
                  l_send, l_recv, own_sem, z_send, z_recv, y_send, y_recv, s_send, s_recv):
    me = lax.axis_index("rows")
    deep = size // 4
    z = me // 4
    core = lax.rem(me, 2)
    mid = lax.rem(me // 2, 2)
    sib = me + 1 - 2 * core
    ynb = me + 2 - 4 * mid
    other = sib + 2 - 4 * mid
    up, down = lax.rem(me + 4, size), lax.rem(me - 4 + size, size)
    pieces = 4
    piece = x_ref.shape[0] // pieces

    def part(block, h):
        return xg_ref.at[block, pl.ds(h * piece, piece)]

    def along(base, k):
        return lax.rem(base + 4 * k + size, size)

    columns, nodes = x_ref.shape
    ones = jnp.ones((local_ref.shape[0] - columns, nodes), bf16)
    x_all = jnp.concatenate([x_ref[...], ones], axis=0)
    turns = 2 * deep
    chunk = nodes // turns

    def local_turns(first, last):
        def turn(i, nothing):
            here = pl.ds(pl.multiple_of(i * chunk, chunk), chunk)
            x_here = jnp.concatenate([x_ref[:, here], ones[:, :chunk]], axis=0)
            local_ref[...] += dot_nn(x_here, dense_ref[here, :])
            local_ref[:, here] += dot_nt(x_all, dense_ref[here, :])
            return nothing

        lax.fori_loop(first, last, turn, 0)

    planes, lines = plane_peers(me), line_peers(me, size)
    peer_barrier(planes + lines)
    plane_copies = send_parts(gram_ref, plane_buf, p_send, p_recv, planes)

    def hop(way, k, h):
        return z_recv.at[way, k, h]

    sends = []

    def send(cond, copy):
        if cond is None:
            copy.start()
        else:
            pl.when(cond)(copy.start)
        sends.append((cond, copy))

    for h in range(pieces):
        src = x_ref.at[pl.ds(h * piece, piece)]
        send(None, remote(src, part(me, h), y_send.at[z, h], y_recv.at[z, h], ynb))
        send(z + 1 < deep, remote(src, part(me, h), z_send.at[0, 0, h], hop(0, 1, h), up))
        send(z > 0, remote(src, part(me, h), z_send.at[1, 0, h], hop(1, 1, h), down))
        send(None, remote(src, part(me, h), s_send.at[0, z, h], s_recv.at[0, z, h], sib))
    own = pltpu.make_async_copy(x_ref, xg_ref.at[me], own_sem)
    own.start()
    local_ref[...] = jnp.zeros_like(local_ref)

    for copy in plane_copies:
        copy.wait()
    half_sum[...] = ordered_sum(lax.rem(me, 4), 4, gram_ref, plane_buf)
    line_copies = send_parts(half_sum, line_buf, l_send, l_recv, lines)

    def take_along_z(k):
        for h in range(pieces):
            for way, there, more, onto in (
                (0, z >= k, z + 1 < deep, up),
                (1, z + k < deep, z > 0, down),
            ):
                offset = -k if way == 0 else k
                block = along(me, offset)
                at = lax.rem(z + offset + deep, deep)
                got = part(block, h)
                pl.when(there)(remote(got, got, z_send.at[way, k, h], hop(way, k, h), onto).wait_recv)
                send(there, remote(got, got, y_send.at[at, h], y_recv.at[at, h], ynb))
                if k + 1 < deep:
                    send(
                        there & more,
                        remote(got, got, z_send.at[way, k, h], hop(way, k + 1, h), onto),
                    )
                send(there, remote(got, got, s_send.at[0, at, h], s_recv.at[0, at, h], sib))

    def take_along_y(k):
        for h in range(pieces):
            for offset, there in ((0, None),) if k == 0 else ((-k, z >= k), (k, z + k < deep)):
                block = along(ynb, offset)
                at = lax.rem(z + offset + deep, deep)
                got = part(block, h)
                wait = remote(got, got, y_send.at[at, h], y_recv.at[at, h], ynb).wait_recv
                if there is None:
                    wait()
                else:
                    pl.when(there)(wait)
                send(there, remote(got, got, s_send.at[1, at, h], s_recv.at[1, at, h], sib))

    n = inv_ref.shape[0]
    rows = lax.broadcasted_iota(jnp.int32, (n, 2 * n), 0)
    lanes = lax.broadcasted_iota(jnp.int32, (n, 2 * n), 1)
    local_turns(0, 2)
    take_along_z(1)
    for copy in line_copies:
        copy.wait()
    gram = unfold(ordered_sum(z, deep, half_sum, line_buf)) / node_total
    unit = jnp.where(rows == lanes, 1.0, 0.0)
    both = jnp.where(lanes < n, unit, jnp.concatenate([gram, gram], axis=1))
    cut = [n * k // deep for k in range(deep + 1)]
    for k in range(1, deep):
        both = back_substitute(n, cut[k - 1], cut[k], both)
        take_along_y(k - 1)
        local_turns(2 * k, 2 * k + 2)
        if k + 1 < deep:
            take_along_z(k + 1)
    both = back_substitute(n, cut[deep - 1], cut[deep], both)
    take_along_y(deep - 1)
    diag = jnp.sum(jnp.where(lanes == rows + n, both, 0.0), axis=1, keepdims=True)
    inv_ref[...] = (both * (1.0 / jnp.sqrt(diag)))[:, :n]

    for at in range(deep):
        for h in range(pieces):
            for line, base in ((0, sib), (1, other)):
                got = part(lax.rem(base, 4) + 4 * at, h)
                remote(got, got, s_send.at[line, at, h], s_recv.at[line, at, h], sib).wait_recv()
    for cond, copy in sends:
        if cond is None:
            copy.wait_send()
        else:
            pl.when(cond)(copy.wait_send)
    own.wait()


def gather_basis(x_bf, gram_part, dense, size, node_total):
    columns, nodes = x_bf.shape
    deep = size // 4
    dma = pltpu.SemaphoreType.DMA
    return pl.pallas_call(
        functools.partial(gather_kernel, size, float(node_total)),
        in_specs=[pl.BlockSpec(memory_space=pltpu.VMEM)] * 3,
        out_specs=[pl.BlockSpec(memory_space=pl.ANY)] + [pl.BlockSpec(memory_space=pltpu.VMEM)] * 2,
        out_shape=[
            jax.ShapeDtypeStruct((size, columns, nodes), bf16),
            jax.ShapeDtypeStruct((columns, columns), f32),
            jax.ShapeDtypeStruct((columns + 16, nodes), f32),
        ],
        scratch_shapes=[
            pltpu.VMEM((4,) + gram_part.shape, f32),
            pltpu.VMEM((deep,) + gram_part.shape, f32),
            pltpu.VMEM(gram_part.shape, f32),
            dma((4,)),
            dma((4,)),
            dma((deep,)),
            dma((deep,)),
            dma,
            dma((2, deep, 4)),
            dma((2, deep, 4)),
            dma((deep, 4)),
            dma((deep, 4)),
            dma((2, deep, 4)),
            dma((2, deep, 4)),
        ],
        compiler_params=pltpu.CompilerParams(
            collective_id=0, has_side_effects=True, vmem_limit_bytes=20 * MIB
        ),
        name="gather_basis",
    )(x_bf, gram_part, dense)


def sum_kernel(size, part_ref, out_ref, plane_buf, line_buf, half_sum, p_send, p_recv, l_send, l_recv):
    me = lax.axis_index("rows")
    planes, lines = plane_peers(me), line_peers(me, size)
    peer_barrier(planes + lines)
    for copy in send_parts(part_ref, plane_buf, p_send, p_recv, planes):
        copy.wait()
    half_sum[...] = ordered_sum(lax.rem(me, 4), 4, part_ref, plane_buf)
    for copy in send_parts(half_sum, line_buf, l_send, l_recv, lines):
        copy.wait()
    out_ref[...] = ordered_sum(me // 4, size // 4, half_sum, line_buf)


def sum_rows(part, size):
    dma = pltpu.SemaphoreType.DMA
    deep = size // 4
    return pl.pallas_call(
        functools.partial(sum_kernel, size),
        in_specs=[pl.BlockSpec(memory_space=pltpu.VMEM)],
        out_specs=pl.BlockSpec(memory_space=pltpu.VMEM),
        out_shape=jax.ShapeDtypeStruct(part.shape, f32),
        scratch_shapes=[
            pltpu.VMEM((4,) + part.shape, f32),
            pltpu.VMEM((deep,) + part.shape, f32),
            pltpu.VMEM(part.shape, f32),
            dma((4,)),
            dma((4,)),
            dma((deep,)),
            dma((deep,)),
        ],
        compiler_params=pltpu.CompilerParams(
            collective_id=1, has_side_effects=True, vmem_limit_bytes=16 * MIB
        ),
        name="sum_rows",
    )(part)


def apply_kernel(first, slots, own_src, own_dst, in_src, in_dst, *refs):
    if first:
        local_ref, own_ref, in_ref, xg_ref, x_ref, image_ref, cross_ref, degree_ref, far = refs
    else:
        local_ref, own_ref, in_ref, xg_ref, x_ref, degree_ref, image_ref, cross_ref, far = refs
    step = pl.program_id(0)
    columns, nodes = x_ref.shape
    rows = far.shape[1]
    edge = own_ref.shape[1]

    def with_ones(x):
        if first:
            return jnp.concatenate([x, jnp.ones((16, x.shape[1]), bf16)], axis=0)
        return x

    @pl.when(step == 0)
    def _():
        far[...] = jnp.zeros_like(far)

    count = own_ref.shape[0]
    blocks = nodes // edge
    for tiles_ref, src_ref, dst_ref, dot in (
        (own_ref, own_src, own_dst, dot_nt),
        (in_ref, in_src, in_dst, dot_nn),
    ):
        products = []
        for t in range(count):
            slot = step * count + t
            at = pl.ds(pl.multiple_of(src_ref[slot] * edge, edge), edge)
            if dot is dot_nt:
                tile = tiles_ref[t]
            else:
                tile = tiles_ref[t // slots, (t % slots) * edge : (t % slots + 1) * edge]
            products.append(dot(with_ones(xg_ref[slot // slots, :, at]), tile))
        for t in range(count):
            far[dst_ref[step * count + t]] += products[t]

    @pl.when(step == pl.num_programs(0) - 1)
    def _():
        for b in range(blocks):
            at = slice(b * edge, (b + 1) * edge)
            both = local_ref[:rows, at] + far[b]
            if first:
                degree = 0.5 * both[columns : columns + 1]
                degree_ref[:, at] = jnp.broadcast_to(degree, (8, edge))
            else:
                degree = degree_ref[:1, at]
            image_ref[:, at] = degree * x_ref[:, at] - 0.5 * both[:columns]
        cross_ref[...] = fold(dot_nt(image_ref[...], x_ref[...], highest))


def apply_operator(first, slots, index, local, own_tiles, in_tiles, xg, x, degree):
    columns, nodes = x.shape
    edge = own_tiles.shape[1]
    steps = 8
    count = own_tiles.shape[0] // steps
    whole = lambda shape: pl.BlockSpec(shape, lambda i, *_: (0,) * len(shape))
    rows = columns + 16 if first else columns
    tile_spec = pl.BlockSpec((count, edge, edge), lambda i, *_: (i, 0, 0))
    degree_shape = (8, nodes)
    in_specs = [
        whole(local.shape),
        tile_spec,
        pl.BlockSpec((count // slots,) + in_tiles.shape[1:], lambda i, *_: (i, 0, 0)),
        whole(xg.shape),
        whole(x.shape),
    ]
    out_specs = [whole(x.shape), whole((columns // 2, 2 * columns))]
    out_shape = [
        jax.ShapeDtypeStruct(x.shape, f32),
        jax.ShapeDtypeStruct((columns // 2, 2 * columns), f32),
    ]
    operands = [local, own_tiles, in_tiles, xg, x]
    if first:
        out_specs.append(whole(degree_shape))
        out_shape.append(jax.ShapeDtypeStruct(degree_shape, f32))
    else:
        in_specs.append(whole(degree_shape))
        operands.append(degree)
    return pl.pallas_call(
        functools.partial(apply_kernel, first, slots),
        grid_spec=pltpu.PrefetchScalarGridSpec(
            num_scalar_prefetch=4,
            grid=(steps,),
            in_specs=in_specs,
            out_specs=out_specs,
            scratch_shapes=[
                pltpu.VMEM((nodes // edge + 1, rows, edge), f32),
            ],
        ),
        out_shape=out_shape,
        compiler_params=pltpu.CompilerParams(vmem_limit_bytes=32 * MIB),
        name="apply_operator",
    )(*index, *operands)


def update_kernel(last, node_total, inv_ref, cross_ref, image_ref, x_ref, degree_ref, *refs):
    inv = inv_ref[...]
    n = inv.shape[0]
    cross = unfold(cross_ref[...]) / node_total
    projected = dot_nt(dot_nn(inv, cross, highest), inv, highest)
    scale = 1.0 / (1.0 + degree_ref[:1, :])
    x = x_ref[...]
    p_inv = dot_nn(projected, inv, highest)
    if last:
        ortho_ref, residual_ref, projected_ref = refs
        ortho_ref[...] = dot_nn(inv, x, highest)
        residual_ref[...] = (dot_nn(inv, image_ref[...], highest) - dot_nn(p_inv, x, highest)) * scale
        projected_ref[...] = projected
    else:
        coeff_ref, dir_ref, x_out, bf_out, dir_out, gram_out = refs
        c_x, c_r, c_p = coeff_ref[:, :n], coeff_ref[:, n : 2 * n], coeff_ref[:, 2 * n :]
        m_image = dot_nn(c_r, inv, highest)
        m_x = dot_nn(c_r, p_inv, highest)
        m_basis = dot_nn(c_x, inv, highest)
        direction = (dot_nn(m_image, image_ref[...], highest) - dot_nn(m_x, x, highest)) * scale
        direction = direction + dot_nn(c_p, dir_ref[...], highest)
        basis = dot_nn(m_basis, x, highest) + direction
        dir_out[...] = direction
        x_out[...] = basis
        bf_out[...] = basis.astype(bf16)
        gram_out[...] = fold(dot_nt(basis, basis, highest))


def update(last, node_total, inv, cross, image, x, degree, coeff=None, direction=None):
    columns, nodes = x.shape
    big = jax.ShapeDtypeStruct((columns, nodes), f32)
    if last:
        shapes = [big, big, jax.ShapeDtypeStruct((columns, columns), f32)]
        operands = (inv, cross, image, x, degree)
    else:
        shapes = [
            big,
            jax.ShapeDtypeStruct((columns, nodes), bf16),
            big,
            jax.ShapeDtypeStruct((columns // 2, 2 * columns), f32),
        ]
        operands = (inv, cross, image, x, degree, coeff, direction)
    vmem = pl.BlockSpec(memory_space=pltpu.VMEM)
    return pl.pallas_call(
        functools.partial(update_kernel, last, float(node_total)),
        in_specs=[vmem] * len(operands),
        out_specs=[vmem] * len(shapes),
        out_shape=shapes,
        compiler_params=pltpu.CompilerParams(vmem_limit_bytes=32 * MIB),
        name="update",
    )(*operands)


def start_kernel(x_ref, bf_out, gram_out):
    x = x_ref[...]
    bf_out[...] = x.astype(bf16)
    gram_out[...] = fold(dot_nt(x, x, highest))


def start(x):
    columns, nodes = x.shape
    vmem = pl.BlockSpec(memory_space=pltpu.VMEM)
    return pl.pallas_call(
        start_kernel,
        in_specs=[vmem],
        out_specs=[vmem] * 2,
        out_shape=[
            jax.ShapeDtypeStruct((columns, nodes), bf16),
            jax.ShapeDtypeStruct((columns // 2, 2 * columns), f32),
        ],
        compiler_params=pltpu.CompilerParams(vmem_limit_bytes=16 * MIB),
        name="start",
    )(x)


def shards(
    local_tiles,
    local_row,
    local_col,
    local_count,
    remote_tiles,
    remote_row,
    remote_col,
    remote_count,
    start_basis,
    start_dir,
    coeffs,
):
    size = lax.axis_size("rows")
    edge = local_tiles.shape[1]
    columns, nodes = start_basis.shape
    blocks = nodes // edge
    slots = remote_tiles.shape[1]
    node_total = nodes * size
    live = jnp.arange(slots)[None, :] < remote_count[:, None]
    numbers = jnp.concatenate([remote_row, jnp.where(live, remote_col, blocks)], axis=1).astype(bf16)
    numbers = jnp.pad(numbers[:, None, :], ((0, 0), (0, 15), (0, edge - 2 * slots)))
    slab = jnp.concatenate([remote_tiles.reshape(size, slots * edge, edge), numbers], axis=1)
    in_tiles = lax.all_to_all(slab, "rows", split_axis=0, concat_axis=0, tiled=True)
    far = in_tiles[:, slots * edge, : 2 * slots].astype(jnp.int32)
    own_tiles = remote_tiles.reshape(-1, edge, edge)
    own_dst = jnp.where(live, remote_row, blocks).reshape(-1)
    index = (
        remote_col.reshape(-1),
        own_dst,
        far[:, :slots].reshape(-1),
        far[:, slots:].reshape(-1),
    )
    dense = dense_local(local_count, local_row, local_col, local_tiles, nodes)
    basis = start_basis
    direction = start_dir
    degree = None
    basis_bf, gram_part = start(basis)
    dense, basis_bf = lax.optimization_barrier((dense, basis_bf))
    passes = coeffs.shape[0]
    for iteration in range(passes + 1):
        xg, inv, local = gather_basis(basis_bf, gram_part, dense, size, node_total)
        out = apply_operator(iteration == 0, slots, index, local, own_tiles, in_tiles, xg, basis, degree)
        image, cross_part = out[:2]
        if iteration == 0:
            degree = out[2]
        cross = sum_rows(cross_part, size)
        if iteration < passes:
            basis, basis_bf, direction, gram_part = update(
                False, node_total, inv, cross, image, basis, degree, coeffs[iteration], direction
            )
    return update(True, node_total, inv, cross, image, basis, degree)


def solution(mesh):
    placed = (
        P(("groups", "rows"), None, None),
        P(("groups", "rows")),
        P(("groups", "rows")),
        P(("groups", "rows")),
        P(("groups", "rows"), None, None, None),
        P(("groups", "rows"), None),
        P(("groups", "rows"), None),
        P(("groups", "rows")),
        P("groups", "rows"),
        P("groups", "rows"),
        P("groups", None, None),
    )
    return jax.shard_map(
        shards,
        mesh=mesh,
        in_specs=placed,
        out_specs=(P("groups", "rows"), P("groups", "rows"), P("groups", None)),
        check_vma=False,
    )
```
